512 devices in a mesh: dp: 128 (over y, z, core), mp: 4 (over x).
Axes of the slice: x: 4, y: 8, z: 8, core: 2. Of those that a mesh axis runs over, the one named last changes fastest.
Arguments:
- hidden: bfloat16 [3072, 4096], P('dp', 'mp')
- adapter_down_weight: bfloat16 [16, 4096], P(None, 'mp'), may hold values from -0.09375 to 0.09375
- adapter_up_weight: bfloat16 [16, 4096], P(None, 'mp'), may hold values from -1.5 to 1.5
- passages: bfloat16 [49152, 4096], P('dp', 'mp')
- candidate_passage_ids: int32 [3072, 8], P('dp'), may hold values from 0 to 49151, as said below
- storage: int32 [49152], replicated, may hold values from 0 to 49151, as said below
Outputs:
- mean_loss: float32 [], replicated
- grad_a: float32 [16, 4096], P(None, 'mp')
- grad_b: float32 [16, 4096], P(None, 'mp')
- grad_passages: bfloat16 [49152, 4096], P('dp', 'mp')
The draws below stay inside these ranges and needn't reach their ends.
Inputs may be any that keep to these rules, and one draw needn't show every extreme that they name: `candidate_passage_ids`: passage ids. The storage row of every listed passage lies with dp index storage row // 384; among the 192 listed passages of each block of 24 queries, at most 3 lie with one dp index, and in every block some index holds exactly 3. Ids may repeat. A permutation: each storage row holds one passage.
All inputs are finite; a program needn't handle non-finite values.
Results may differ from the reference program's by a relative error of at most 0.0081.
Values may be sent and summed in bfloat16 or wider, within the bound.
A program may use at most 64 MiB of HBM per device.

```python
import math
import jax
import jax.numpy as jnp
from jax import lax

EMBED_WIDTH = 4096
LOW_RANK_SIZE = 16
LISTED = 8
Q_DEV = 24
P_DEV = 384
QUERIES = 3072
PASSAGES = 49152
N_DP = 128


def storage_order(key):
    return jax.random.permutation(jax.random.fold_in(key, 11), PASSAGES).astype(jnp.int32)


def listed_ids(key):
    order = storage_order(key)
    holder = jnp.argsort(order).astype(jnp.int32)
    keys = jax.random.split(jax.random.fold_in(key, 12), 4)
    block_rows = Q_DEV * LISTED
    capacity = 2 * block_rows // N_DP
    remainder = block_rows - capacity
    hottest = jax.random.randint(keys[0], (N_DP, 1), 0, N_DP)
    position = jnp.arange(block_rows, dtype=jnp.int32)[None, :] - capacity
    jitter = jax.random.randint(keys[1], (N_DP, block_rows), 0, remainder)
    offsets = jnp.where(position < 0, 0, 1 + (jnp.maximum(position, 0) * (N_DP - 2) + jitter) // remainder)
    owners = (hottest + offsets) % N_DP

    def shuffle_one(subkey):
        return jax.random.permutation(subkey, block_rows)
    shuffle = jax.vmap(shuffle_one)(jax.random.split(keys[2], N_DP))
    owners = jnp.take_along_axis(owners, shuffle, axis=1)
    local_rows = jax.random.randint(keys[3], (N_DP, block_rows), 0, P_DEV)
    return holder[owners * P_DEV + local_rows].reshape(QUERIES, LISTED)


def passage_parts(key):
    keys = jax.random.split(jax.random.fold_in(key, 21), 2)
    uniforms = jax.random.uniform(keys[0], (PASSAGES, EMBED_WIDTH), jnp.float32, 0.0005, 0.9995)
    levels = jax.random.uniform(keys[1], (PASSAGES, 1), jnp.float32)
    return (uniforms, levels)


def draw_storage(key, part):
    return storage_order(key)


def draw_candidate_passage_ids(key, part):
    return listed_ids(key)


def draw_passages(key, part):
    uniforms, levels = passage_parts(key)
    table = 1.4142136 * lax.erf_inv(uniforms * 2.0 - 1.0) * jnp.exp(levels * 1.4 - 0.7) / 64.0
    return table.astype(jnp.bfloat16)


def draw_hidden(key, part):
    inner = jax.random.split(jax.random.fold_in(key, 31), 1)
    states = jax.random.normal(inner[0], (QUERIES, EMBED_WIDTH), jnp.float32)
    return states.astype(jnp.bfloat16)


def shard_levels(key, dims, pieces, low, top_value):
    gain, own = 1.0, jax.random.fold_in(key, 6)
    for axis_at, parts in pieces:
        steps = jnp.exp(jax.random.uniform(jax.random.fold_in(own, axis_at), (parts,), jnp.float32, low / len(pieces), top_value / len(pieces)))
        gain = gain * jnp.repeat(steps, dims[axis_at] // parts).reshape([-1 if axis == axis_at else 1 for axis in range(len(dims))])
    return gain


def noise(own_key, extent, scale, most, pieces=(), kind=jnp.bfloat16):
    drawn = jax.random.normal(own_key, extent, jnp.float32) * scale
    if len(pieces) > 0:
        drawn = shard_levels(own_key, extent, pieces, -0.22, 0.18) * drawn
    return jnp.clip(drawn, min=-most, max=most).astype(kind)


def setup_inputs(seed: int = 0) -> dict:
    arg_keys = jax.random.split(jax.random.key(seed), 7)
    return {
        "hidden": draw_hidden(jax.random.fold_in(arg_keys[6], 71), 0),
        "adapter_down_weight": noise(arg_keys[1], (LOW_RANK_SIZE, EMBED_WIDTH), EMBED_WIDTH ** -0.5, 0.09375, ((1, 4),)),
        "adapter_up_weight": noise(arg_keys[2], (LOW_RANK_SIZE, EMBED_WIDTH), LOW_RANK_SIZE ** -0.5, 1.5, ((1, 4),)),
        "passages": draw_passages(jax.random.fold_in(arg_keys[6], 71), 0),
        "candidate_passage_ids": draw_candidate_passage_ids(jax.random.fold_in(arg_keys[6], 71), 0),
        "storage": draw_storage(jax.random.fold_in(arg_keys[6], 71), 0),
    }


SOFTMAX_TEMPER = 0.02
EPSILON = 1e-06

def contracted_rows(first_op, second_op):
    return lax.dot_general(first_op, second_op, (((1,), (1,)), ((), ())), preferred_element_type=jnp.float32)

def contract_cols(first_op, second_op):
    return lax.dot_general(first_op, second_op, (((0,), (0,)), ((), ())), preferred_element_type=jnp.float32)

def reference(hidden, adapter_down_weight, adapter_up_weight, passages, candidate_passage_ids, storage):
    block_rows = Q_DEV * LISTED
    logit_scale = 1.0 / (SOFTMAX_TEMPER * math.sqrt(EMBED_WIDTH))
    located_all = jnp.take(storage, candidate_passage_ids, axis=0)
    positive_cols = jnp.arange(Q_DEV, dtype=jnp.int32) * LISTED

    def one_block(carry, block_index):
        table_grad, grad_a, grad_b, loss_total = carry
        start_row = (block_index * Q_DEV).astype(jnp.int32)
        hidden_state_rows = lax.dynamic_slice_in_dim(hidden, start_row, Q_DEV, 0)
        located = lax.dynamic_slice_in_dim(located_all, start_row, Q_DEV, 0).reshape(block_rows)
        reduced_projection = contracted_rows(hidden_state_rows, adapter_down_weight).astype(jnp.bfloat16)
        combined_rows = hidden_state_rows.astype(jnp.float32) + jnp.dot(reduced_projection, adapter_up_weight, preferred_element_type=jnp.float32)
        inverse_norm = lax.rsqrt(lax.optimization_barrier(jnp.mean(combined_rows * combined_rows, axis=1, keepdims=True)) + EPSILON)
        query_wide = combined_rows * inverse_norm
        query_half = query_wide.astype(jnp.bfloat16)
        candidates = jnp.take(passages, located, axis=0)
        scores = contracted_rows(query_half, candidates) * logit_scale
        row_max = lax.optimization_barrier(jnp.max(scores, axis=1, keepdims=True))
        exponent = jnp.exp(scores - row_max)
        totals = lax.optimization_barrier(jnp.sum(exponent, axis=1, keepdims=True))
        columns = lax.broadcasted_iota(jnp.int32, scores.shape, 1)
        picked = (columns == positive_cols[:, None]).astype(jnp.float32)
        loss_rows = jnp.log(totals[:, 0]) + row_max[:, 0] - lax.optimization_barrier(jnp.sum(scores * picked, axis=1))
        weights = ((exponent / totals - picked) * logit_scale).astype(jnp.bfloat16)
        query_grad = jnp.dot(weights, candidates, preferred_element_type=jnp.float32)
        cand_grad = contract_cols(weights, query_half).astype(jnp.bfloat16)
        table_grad = table_grad.at[located].add(cand_grad.astype(jnp.float32))
        tangent = lax.optimization_barrier(jnp.mean(query_wide * query_grad, axis=1, keepdims=True))
        combined_gradient = (inverse_norm * (query_grad - query_wide * tangent)).astype(jnp.bfloat16)
        grad_b = grad_b + contract_cols(reduced_projection, combined_gradient)
        reduced_gradient = contracted_rows(combined_gradient, adapter_up_weight).astype(jnp.bfloat16)
        grad_a = grad_a + contract_cols(reduced_gradient, hidden_state_rows)
        loss_total = loss_total + jnp.sum(loss_rows)
        return ((table_grad, grad_a, grad_b, loss_total), None)
    initial = (jnp.zeros((PASSAGES, EMBED_WIDTH), jnp.float32), jnp.zeros((LOW_RANK_SIZE, EMBED_WIDTH), jnp.float32), jnp.zeros((LOW_RANK_SIZE, EMBED_WIDTH), jnp.float32), jnp.zeros((), jnp.float32))
    block_list = jnp.arange(QUERIES // Q_DEV, dtype=jnp.int32)
    finals, unused = lax.scan(one_block, initial, block_list)
    table_grad, grad_a, grad_b, loss_total = finals
    return (loss_total / QUERIES, grad_a, grad_b, table_grad.astype(jnp.bfloat16))
```

```python
import functools
import math

import jax
import jax.numpy as jnp
from jax import lax
from jax.experimental import pallas as pl
from jax.experimental.pallas import tpu as pltpu
from jax.sharding import PartitionSpec as P

SOFTMAX_TEMPER = 0.02
EPSILON = 1e-06
MESH = pl.DeviceIdType.MESH
F32, BF16 = jnp.float32, jnp.bfloat16
SLOTS = 3
NY = NZ = 8
NX = 4
Q = 24
LISTED = 8
CHIP = 2 * Q
RANK = 16
ROWS = 384
WIDTH = 1024
HALF = WIDTH // 2
DEVS = 2 * NY * NZ
GROUP = NZ * CHIP
VOFF = SLOTS * Q
G_LANE, LOSS_LANE = 120, 121
TINY = 2.0**-80
NEG = -1e38


def nn(a, b):
    return lax.dot_general(a, b, (((1,), (0,)), ((), ())), preferred_element_type=F32)


def nt(a, b):
    return lax.dot_general(a, b, (((1,), (1,)), ((), ())), preferred_element_type=F32)


def tn(a, b):
    return lax.dot_general(a, b, (((0,), (0,)), ((), ())), preferred_element_type=F32)


def exact(dims, a, b):
    return lax.dot_general(a, b, (dims, ((), ())), preferred_element_type=F32, precision=lax.Precision.HIGHEST)


def split(x, parts):
    out = []
    for _ in range(parts):
        top = x.astype(BF16)
        out.append(top)
        x = x - top.astype(F32)
    return out


def iota(shape, dim):
    return lax.broadcasted_iota(jnp.int32, shape, dim)


def kernel(
    ids_ref, hidden_ref, down_ref, up_ref, pass_ref, storage_ref,
    loss_ref, ga_ref, gb_ref, table_ref,
    hbuf, mine, theirs, xb1, xb2, locs, lists, pick, picked, folds, diag, rsx, part, summed, got, back, wrec,
    cand, piece_out, piece_in, piece_sum, final, mixed_ref,
    st_sem, e1_sem, e2_sem, l_sem, lz_sem, ly_sem, ring_sem, sib_sem, rsx_sem, got_sem, w_sem, rs_sem, ag_sem,
    send_sem, small_sem,
):
    me, mp = lax.axis_index("dp"), lax.axis_index("mp")
    core, chip_me = lax.rem(me, 2), me // 2
    y, z = chip_me // NZ, lax.rem(chip_me, NZ)

    def dev(yy, zz, c):
        return ((lax.rem(yy + NY, NY) * NZ + lax.rem(zz + NZ, NZ)) * 2 + c, mp)

    def push(src, dst, ssem, rsem, target):
        pltpu.make_async_remote_copy(
            src_ref=src, dst_ref=dst, send_sem=ssem, recv_sem=rsem, device_id=target, device_id_type=MESH
        ).start()

    def take(ref, sem):
        pltpu.make_async_copy(ref, ref, sem).wait()

    sibling = (chip_me * 2 + 1 - core, mp)

    bar = pltpu.get_barrier_semaphore()
    for t in (dev(y + 1, z, core), dev(y - 1, z, core), dev(y, z + 1, core), dev(y, z - 1, core), sibling):
        pl.semaphore_signal(bar, inc=1, device_id=t, device_id_type=MESH)
    for i in range(1, NX):
        pl.semaphore_signal(bar, inc=1, device_id=(me, lax.rem(mp + i, NX)), device_id_type=MESH)

    hid32 = hidden_ref[...].astype(F32)
    up32 = up_ref[...].astype(F32)
    mine[...] = jnp.concatenate([hid32, jnp.zeros((8, WIDTH), F32)], axis=0).astype(BF16)
    left = jnp.concatenate([hid32, up32], axis=0).astype(BF16)
    right = jnp.concatenate([down_ref[...].astype(F32), up32, jnp.zeros((96, WIDTH), F32)], axis=0).astype(BF16)
    prod = nt(left, right)
    biggest = jnp.max(jnp.max(jnp.abs(pass_ref[...].astype(F32)), axis=0, keepdims=True), axis=1, keepdims=True)
    lane40, row40 = iota((40, 128), 1), iota((40, 128), 0)
    xb1[mp] = jnp.where((lane40 == 40) & (row40 == 0), biggest, prod)

    pl.semaphore_wait(bar, 5 + NX - 1)
    push(mine, theirs, small_sem.at[0], st_sem, sibling)
    for i in range(1, NX):
        push(xb1.at[mp], xb1.at[mp], small_sem.at[1], e1_sem, (me, lax.rem(mp + i, NX)))

    lane1 = iota((1, 128), 1)
    for j in range(Q * LISTED):
        pid = ids_ref[j // LISTED, j % LISTED]
        row = storage_ref[pl.ds(pid // 128, 1), :]
        locs[pl.ds(j, 1), :] = jnp.where(lane1 == lax.rem(pid, 128), row, 0).astype(F32)
    located = jnp.sum(locs[...], axis=1, keepdims=True)
    located = jnp.concatenate([located, jnp.full((64, 1), 1e6, F32)], axis=0)
    r256, l256 = iota((256, 256), 0), iota((256, 256), 1)
    as_row = jnp.sum(jnp.where(r256 == l256, located, 0.0), axis=0, keepdims=True)
    lists[0, pl.ds(me, 1), :] = as_row[:, 0:128]
    lists[1, pl.ds(me, 1), :] = as_row[:, 128:256]
    push(lists.at[:, pl.ds(me, 1), :], lists.at[:, pl.ds(me, 1), :], small_sem.at[2], l_sem, sibling)

    take(theirs, st_sem)
    theirs32 = theirs[0:Q, :].astype(F32)
    both = jnp.where(core == 0, jnp.concatenate([hid32, theirs32], axis=0), jnp.concatenate([theirs32, hid32], axis=0))
    hbuf[pl.ds(pl.multiple_of(chip_me * CHIP, 16), CHIP), :] = both.astype(BF16)

    sa, sb = NZ - (NZ - 1) * core, 1 + (NZ - 1) * core
    a = jnp.where(core == 0, y, z)
    b = jnp.where(core == 0, z, y)
    lanes = pl.ds(pl.multiple_of(core * HALF, HALF), HALF)

    def chip_of(aa, bb):
        return lax.rem(aa + 2 * NY, NY) * sa + lax.rem(bb + 2 * NY, NY) * sb

    def region(ci):
        return hbuf.at[pl.ds(pl.multiple_of(ci * CHIP, 16), CHIP), lanes]

    def pass_on(ci, target, rsem):
        push(region(ci), region(ci), send_sem, rsem, target)

    ar, al = (chip_of(a + 1, b) * 2 + core, mp), (chip_of(a - 1, b) * 2 + core, mp)
    br, bl = (chip_of(a, b + 1) * 2 + core, mp), (chip_of(a, b - 1) * 2 + core, mp)
    order = [0, -1, 1, -2, 2, -3, 3, -4]

    def steps(j, d):
        return 4 if (j % 2 == 0) == (d > 0) else 3

    def event(j, t):
        off = order[j]
        if t == 0:
            ci = chip_of(a + off, b)
            if j > 0:
                take(region(ci), ring_sem.at[ci])
            if j == 0 or (off < 0 and off > -4):
                pass_on(ci, ar, ring_sem.at[ci])
            if j == 0 or (off > 0 and off < 3):
                pass_on(ci, al, ring_sem.at[ci])
            pass_on(ci, br, ring_sem.at[ci])
            pass_on(ci, bl, ring_sem.at[ci])
            if j > 0:
                pass_on(ci, sibling, sib_sem.at[ci])
        else:
            for d in (1, -1):
                if t <= steps(j, d):
                    ci = chip_of(a + off, b - d * t)
                    take(region(ci), ring_sem.at[ci])
                    if t < steps(j, d):
                        pass_on(ci, br if d > 0 else bl, ring_sem.at[ci])
                    pass_on(ci, sibling, sib_sem.at[ci])

    event(0, 0)

    take(xb1.at[pl.ds(0, NX - 1)], e1_sem)
    tot = xb1[0] + xb1[1] + xb1[2] + xb1[3]
    most = jnp.maximum(jnp.maximum(xb1[0], xb1[1]), jnp.maximum(xb1[2], xb1[3]))
    most = jnp.max(jnp.where((lane40 == 40) & (row40 == 0), most, 0.0))
    shrink = jnp.where(most > 2.0**40, TINY, 1.0)
    low_half = tot[0:Q, 0:RANK].astype(BF16)
    rolled = pltpu.roll(tot, 128 - RANK, 1)
    hid_up, gram = rolled[0:Q, 0:RANK], rolled[Q : Q + RANK, 0:RANK]
    mixed = hid32 + nn(low_half, up_ref[...])
    mixed_ref[...] = mixed
    xb2[mp] = jnp.broadcast_to(jnp.sum(mixed * mixed, axis=1, keepdims=True), (Q, 128))
    for i in range(1, NX):
        push(xb2.at[mp], xb2.at[mp], small_sem.at[3], e2_sem, (me, lax.rem(mp + i, NX)))

    take(lists.at[:, pl.ds(0, 1), :], l_sem)

    def line(ref_rows, n):
        return lists.at[:, pl.ds(ref_rows, n), :]

    zr, zl = dev(y, z + 1, core), dev(y, z - 1, core)
    yr, yl = dev(y + 1, z, core), dev(y - 1, z, core)

    def list_step(t):
        if t <= 4:
            for d, to in ((1, zr), (-1, zl)):
                lim = 4 if d > 0 else 3
                if t > lim:
                    continue
                zz = lax.rem(z - d * t + 2 * NZ, NZ)
                rows = pl.multiple_of((y * NZ + zz) * 2, 2)
                if t > 0:
                    take(line(rows, 2), lz_sem.at[zz])
                if t < lim:
                    push(line(rows, 2), line(rows, 2), small_sem.at[4], lz_sem.at[zz], to)
        if t >= 4:
            u = t - 4
            for d, to in ((1, yr), (-1, yl)):
                lim = 4 if d > 0 else 3
                if u > lim:
                    continue
                yy = lax.rem(y - d * u + 2 * NY, NY)
                rows = pl.multiple_of(yy * 2 * NZ, 2 * NZ)
                if u > 0:
                    take(line(rows, 2 * NZ), ly_sem.at[yy])
                if u < lim:
                    push(line(rows, 2 * NZ), line(rows, 2 * NZ), small_sem.at[5], ly_sem.at[yy], to)

    list_step(0)

    events = sorted((j + 2 * t, t, j) for j in range(8) for t in range(5) if j + t > 0)
    sections = {}
    for n, (key, t, j) in enumerate(events):
        event(j, t)
        if n % 4 == 3 and n // 4 + 1 <= 8:
            list_step(n // 4 + 1)

    take(xb2.at[pl.ds(0, NX - 1)], e2_sem)
    inv_norm = lax.rsqrt((xb2[0] + xb2[1] + xb2[2] + xb2[3]) / (WIDTH * NX) + EPSILON)

    wanted = jnp.concatenate([lists[0], lists[1]], axis=1) - (me * ROWS).astype(F32)
    here = (wanted >= 0.0) & (wanted < ROWS)
    earlier = nn(here.astype(F32).astype(BF16), (r256 < l256).astype(F32).astype(BF16))
    rows_iota = iota((DEVS, ROWS), 1).astype(F32)
    group_mask = (iota((SLOTS * 16, GROUP), 1) // Q) == lax.rem(iota((SLOTS * 16, GROUP), 0), 16)
    part_pu = jnp.zeros((DEVS, 128), F32)
    for s in range(SLOTS):
        col = jnp.sum(jnp.where(here & (earlier == s), wanted + 1.0, 0.0), axis=1, keepdims=True) - 1.0
        pk = (rows_iota == col).astype(F32).astype(BF16)
        pick[s] = pk
        picked[s] = (nn(pk, pass_ref[...]) * shrink).astype(BF16)
        f_lane = iota((GROUP, 128), 1) - s * Q
        folds[s] = ((f_lane == lax.rem(iota((GROUP, 128), 0), Q)) & (f_lane >= 0)).astype(F32).astype(BF16)
        up_at = jnp.concatenate(
            [jnp.zeros((VOFF + s * RANK, WIDTH), F32), up32, jnp.zeros((128 - VOFF - (s + 1) * RANK, WIDTH), F32)], axis=0
        ).astype(BF16)
        part_pu = part_pu + nt(picked[s], up_at)

    owner = jnp.floor((located + 0.5) * (1.0 / ROWS))
    hold = (iota((256, 128), 1).astype(F32) == owner).astype(F32)
    hold_b = hold.astype(BF16)
    rank = jnp.sum(hold * nn((r256 > l256).astype(F32).astype(BF16), hold_b), axis=1, keepdims=True)
    count = tn(hold_b, jnp.ones((256, 128), BF16))
    l_col = iota((256, 128), 1)
    pos_at = (iota((256, 128), 0) == LISTED * lax.rem(l_col, Q)) & (rank == (l_col // Q).astype(F32)) & (l_col < VOFF)
    positive = tn(hold_b, pos_at.astype(F32).astype(BF16))
    lane = iota((DEVS, 128), 1)
    valid = (count > (lane // Q).astype(F32)) & (lane < VOFF)

    row128 = iota((128, RANK), 0)
    at_rank = ((row128 >= VOFF) & (row128 < VOFF + SLOTS * RANK) & (lax.rem(row128 - VOFF + 128 * RANK, RANK) == iota((128, RANK), 1)))
    at_rank = at_rank.astype(F32)
    at_query = ((iota((Q, 128), 1) < VOFF) & (lax.rem(iota((Q, 128), 1), Q) == iota((Q, 128), 0))).astype(F32)
    spread = nn(nt(at_rank.astype(BF16), low_half).astype(BF16), at_query.astype(BF16))
    row_a, lane_a = iota((128, 128), 0), iota((128, 128), 1)
    same_slot = ((row_a + 128 * RANK - VOFF) // RANK - 128) == lane_a // Q
    spread = jnp.where(same_slot, spread, 0.0).astype(BF16)
    inv_lane = jnp.sum(inv_norm * at_query, axis=0, keepdims=True)

    def rest(i, c):
        @pl.when(i != chip_me)
        def _():
            r = hbuf.at[pl.ds(pl.multiple_of(i * CHIP, 16), CHIP), pl.ds(pl.multiple_of(HALF - core * HALF, HALF), HALF)]
            take(r, sib_sem.at[i])
        return c

    lax.fori_loop(0, NY * NZ, rest, 0)

    def score(g, c):
        rows = pl.ds(pl.multiple_of(g * 16, 16), 16)
        s_g = jnp.concatenate([picked[s, rows, :] for s in range(SLOTS)], axis=0)
        d = nt(s_g, hbuf[pl.ds(pl.multiple_of(g * GROUP, 16), GROUP), :])
        d = jnp.where(group_mask, d, 0.0)
        acc = jnp.zeros((16, 128), F32)
        for s in range(SLOTS):
            for piece in split(d[s * 16 : (s + 1) * 16, :], 3):
                acc = acc + nn(piece, folds[s])
        part[rows, :] = acc
        return c

    lax.fori_loop(0, NY, score, 0)
    part[...] = part[...] + part_pu + jnp.where(lane == G_LANE, shrink * (1.0 / NX), 0.0)

    quarter = DEVS // NX

    def q_rows(k):
        return part.at[pl.ds(pl.multiple_of(k * quarter, quarter), quarter), :]

    for i in range(1, NX):
        k = lax.rem(mp + i, NX)
        push(q_rows(k), rsx.at[mp], small_sem.at[6], rsx_sem, (me, k))
    rsx[mp] = part[pl.ds(pl.multiple_of(mp * quarter, quarter), quarter), :]
    take(rsx.at[pl.ds(0, NX - 1)], rsx_sem)
    summed[...] = rsx[0] + rsx[1] + rsx[2] + rsx[3]

    def give(i, c):
        j = lax.rem(i + me, quarter)
        block = mp * quarter + j
        for dk in range(NX):
            k = lax.rem(mp + dk, NX)
            src = summed.at[pl.ds(j, 1), :]
            if dk == 0:
                @pl.when(block == me)
                def _():
                    pltpu.make_async_copy(src, got.at[pl.ds(me, 1), :], got_sem).start()

                @pl.when(block != me)
                def _():
                    push(src, got.at[pl.ds(me, 1), :], small_sem.at[7], got_sem, (block, k))
            else:
                push(src, got.at[pl.ds(me, 1), :], small_sem.at[7], got_sem, (block, k))
        return c

    lax.fori_loop(0, quarter, give, 0)
    take(got, got_sem)

    g = got[...]
    unshrink = jnp.sum(jnp.where(lane == G_LANE, g, 0.0), axis=1, keepdims=True)
    unshrink = jnp.where(unshrink < 0.5, 1.0 / TINY, 1.0)
    ranks = jnp.where((lane >= VOFF) & (lane < VOFF + SLOTS * RANK), g, 0.0)
    raw = g
    for piece in split(ranks, 3):
        raw = raw + nn(piece, spread)
    raw = jnp.where(valid & (inv_lane > 0.0), raw * inv_lane * unshrink, 0.0)
    scale = 1.0 / (SOFTMAX_TEMPER * math.sqrt(WIDTH * NX))
    scores = jnp.where(valid, raw * scale, NEG)

    def over_slots(x, op, fill):
        x0 = op(op(x, pltpu.roll(x, 128 - Q, 1)), pltpu.roll(x, 128 - 2 * Q, 1))
        return jnp.where(lane1 < Q, x0, jnp.where(lane1 < 2 * Q, pltpu.roll(x0, Q, 1), jnp.where(lane1 < 3 * Q, pltpu.roll(x0, 2 * Q, 1), fill)))

    top = over_slots(jnp.max(scores, axis=0, keepdims=True), jnp.maximum, 0.0)
    expo = jnp.where(valid, jnp.exp(scores - top), 0.0)
    total = over_slots(jnp.sum(expo, axis=0, keepdims=True), jnp.add, 1.0)
    own = over_slots(jnp.sum(jnp.where(positive > 0.5, scores, 0.0), axis=0, keepdims=True), jnp.add, 0.0)
    loss = jnp.sum(jnp.where(lane1 < Q, jnp.log(total) + top - own, 0.0), axis=1, keepdims=True)
    weights = jnp.where(valid, (expo / total - positive) * scale, 0.0)
    tangent = over_slots(jnp.sum(weights * raw, axis=0, keepdims=True), jnp.add, 0.0) / (WIDTH * NX)
    w2 = weights * inv_lane
    v = jnp.zeros((DEVS, 128), F32)
    for piece in split(w2, 3):
        v = v + nt(piece, spread)
    back[...] = w2 + v + jnp.where(lane == LOSS_LANE, loss, 0.0)

    def hand(i, c):
        t = lax.rem(me + 1 + i, DEVS)
        push(back.at[pl.ds(t, 1), :], wrec.at[pl.ds(me, 1), :], small_sem.at[8], w_sem, (t, mp))
        return c

    lax.fori_loop(0, DEVS - 1, hand, 0)
    pltpu.make_async_copy(back.at[pl.ds(me, 1), :], wrec.at[pl.ds(me, 1), :], w_sem).start()

    z_all = exact(((0,), (0,)), weights, ranks * unshrink)
    z_all = jnp.where(lane_a >= VOFF, z_all, 0.0)
    same_t = ((lane_a + 128 * RANK - VOFF) // RANK - 128) == row_a // Q
    z_all = jnp.where(same_t, z_all, 0.0)
    w_pu = exact(((1,), (0,)), exact(((1,), (0,)), at_query, z_all), at_rank)
    inv_col = inv_norm[:, 0:1]
    q_up = inv_col * (hid_up + exact(((1,), (0,)), low_half.astype(F32), gram))
    tan_col = jnp.sum(jnp.where((iota((Q, 128), 1) < Q), at_query, 0.0) * tangent, axis=1, keepdims=True)
    low_grad = (inv_col * (w_pu - tan_col * q_up)).astype(BF16)
    ga = tn(low_grad, hidden_ref[...])
    pulled = (mixed_ref[...] * (inv_col * inv_col * tan_col)).astype(BF16)
    gb = -tn(low_half, pulled)

    take(wrec, w_sem)
    w = wrec[...]
    loss_ref[...] = jnp.broadcast_to(jnp.sum(jnp.where(lane == LOSS_LANE, w, 0.0)) / (DEVS * Q), (8, 128))
    w_t = jnp.transpose(w)
    for s in range(SLOTS):
        for piece in split(w_t[VOFF + s * RANK : VOFF + (s + 1) * RANK, :], 2):
            gb = gb + nn(piece, picked[s]) * (1.0 / shrink)
    for j in range(WIDTH // 128):
        piece_out[0, pl.ds(j * RANK, RANK), :] = ga[:, j * 128 : (j + 1) * 128]
        piece_out[1, pl.ds(j * RANK, RANK), :] = gb[:, j * 128 : (j + 1) * 128]

    def strew(i, c):
        t = lax.rem(me + 1 + i, DEVS)
        push(piece_out.at[:, pl.ds(t, 1), :], piece_in.at[:, pl.ds(me, 1), :], small_sem.at[9], rs_sem, (t, mp))
        return c

    lax.fori_loop(0, DEVS - 1, strew, 0)
    pltpu.make_async_copy(piece_out.at[:, pl.ds(me, 1), :], piece_in.at[:, pl.ds(me, 1), :], rs_sem).start()

    hi, lo = split(w, 2)
    wide = (iota((DEVS, GROUP), 1) // Q) == lax.rem(iota((DEVS, GROUP), 0), 16)
    for s in range(SLOTS):
        diag[0, s] = jnp.where(wide, nt(hi, folds[s]), 0.0).astype(BF16)
        diag[1, s] = jnp.where(wide, nt(lo, folds[s]), 0.0).astype(BF16)

    def candidates(g_, c):
        rows = pl.ds(pl.multiple_of(g_ * 16, 16), 16)
        d = jnp.concatenate([diag[h, s, rows, :] for h in (0, 1) for s in range(SLOTS)], axis=0)
        o = nn(d, hbuf[pl.ds(pl.multiple_of(g_ * GROUP, 16), GROUP), :])
        o = o[0:48, :] + o[48:96, :]
        for s in range(SLOTS):
            cand[s, rows, :] = o[s * 16 : (s + 1) * 16, :]
        return c

    lax.fori_loop(0, NY, candidates, 0)
    table = jnp.zeros((ROWS, WIDTH), F32)
    for s in range(SLOTS):
        up_at = jnp.concatenate(
            [jnp.zeros((VOFF + s * RANK, WIDTH), F32), up32, jnp.zeros((128 - VOFF - (s + 1) * RANK, WIDTH), F32)], axis=0
        ).astype(BF16)
        cg = (cand[s] + nn(hi, up_at) + nn(lo, up_at)).astype(BF16)
        table = table + tn(pick[s], cg)
    table_ref[...] = table.astype(BF16)

    take(piece_in, rs_sem)
    piece_sum[...] = jnp.sum(piece_in[...], axis=1, keepdims=True)
    final[:, pl.ds(me, 1), :] = piece_sum[...]

    def share(i, c):
        t = lax.rem(me + 1 + i, DEVS)
        push(piece_sum, final.at[:, pl.ds(me, 1), :], small_sem.at[10], ag_sem, (t, mp))
        return c

    lax.fori_loop(0, DEVS - 1, share, 0)
    take(final.at[:, pl.ds(0, DEVS - 1), :], ag_sem)
    for j in range(WIDTH // 128):
        ga_ref[:, pl.ds(j * 128, 128)] = final[0, pl.ds(j * RANK, RANK), :]
        gb_ref[:, pl.ds(j * 128, 128)] = final[1, pl.ds(j * RANK, RANK), :]

    take(hbuf.at[pl.ds(0, (NY * NZ - 1) * CHIP), :], send_sem)
    take(mine, small_sem.at[0])
    take(xb1.at[pl.ds(0, NX - 1)], small_sem.at[1])
    take(lists.at[:, pl.ds(0, 1), :], small_sem.at[2])
    take(xb2.at[pl.ds(0, NX - 1)], small_sem.at[3])
    take(lists.at[:, pl.ds(0, 2 * 7), :], small_sem.at[4])
    take(lists.at[:, pl.ds(0, 2 * NZ * 7), :], small_sem.at[5])
    take(rsx.at[pl.ds(0, NX - 1)], small_sem.at[6])
    home = (me // quarter) == mp

    @pl.when(home)
    def _():
        take(got.at[pl.ds(0, DEVS - 1), :], small_sem.at[7])

    @pl.when(jnp.logical_not(home))
    def _():
        take(got, small_sem.at[7])

    take(wrec.at[pl.ds(0, DEVS - 1), :], small_sem.at[8])
    take(piece_in.at[:, pl.ds(0, DEVS - 1), :], small_sem.at[9])
    take(final.at[:, pl.ds(0, DEVS - 1), :], small_sem.at[10])


def shards(hidden, down, up, passages, ids, storage):
    vm = pl.BlockSpec(memory_space=pltpu.VMEM)
    dma = pltpu.SemaphoreType.DMA
    loss, ga, gb, table = pl.pallas_call(
        kernel,
        out_shape=(
            jax.ShapeDtypeStruct((8, 128), F32),
            jax.ShapeDtypeStruct((RANK, WIDTH), F32),
            jax.ShapeDtypeStruct((RANK, WIDTH), F32),
            jax.ShapeDtypeStruct((ROWS, WIDTH), BF16),
        ),
        in_specs=[pl.BlockSpec(memory_space=pltpu.SMEM), vm, vm, vm, vm, vm],
        out_specs=(vm, vm, vm, vm),
        scratch_shapes=[
            pltpu.VMEM((DEVS * Q, WIDTH), BF16),
            pltpu.VMEM((32, WIDTH), BF16),
            pltpu.VMEM((32, WIDTH), BF16),
            pltpu.VMEM((NX, 40, 128), F32),
            pltpu.VMEM((NX, Q, 128), F32),
            pltpu.VMEM((Q * LISTED, 128), F32),
            pltpu.VMEM((2, DEVS, 128), F32),
            pltpu.VMEM((SLOTS, DEVS, ROWS), BF16),
            pltpu.VMEM((SLOTS, DEVS, WIDTH), BF16),
            pltpu.VMEM((SLOTS, GROUP, 128), BF16),
            pltpu.VMEM((2, SLOTS, DEVS, GROUP), BF16),
            pltpu.VMEM((NX, DEVS // NX, 128), F32),
            pltpu.VMEM((DEVS, 128), F32),
            pltpu.VMEM((DEVS // NX, 128), F32),
            pltpu.VMEM((DEVS, 128), F32),
            pltpu.VMEM((DEVS, 128), F32),
            pltpu.VMEM((DEVS, 128), F32),
            pltpu.VMEM((SLOTS, DEVS, WIDTH), F32),
            pltpu.VMEM((2, DEVS, 128), F32),
            pltpu.VMEM((2, DEVS, 128), F32),
            pltpu.VMEM((2, 1, 128), F32),
            pltpu.VMEM((2, DEVS, 128), F32),
            pltpu.VMEM((Q, WIDTH), F32),
            dma, dma, dma, dma,
            dma((NZ,)), dma((NY,)),
            dma((NY * NZ,)), dma((NY * NZ,)),
            dma, dma, dma, dma, dma,
            dma, dma((11,)),
        ],
        compiler_params=pltpu.CompilerParams(collective_id=0, has_side_effects=True, vmem_limit_bytes=56 << 20),
        name="contrastive",
    )(ids, hidden, down, up, passages, storage.reshape(ROWS, 128))
    return loss[0, 0], ga, gb, table


def solution(mesh):
    return jax.shard_map(
        shards,
        mesh=mesh,
        in_specs=(P("dp", "mp"), P(None, "mp"), P(None, "mp"), P("dp", "mp"), P("dp", None), P()),
        out_specs=(P(), P(None, "mp"), P(None, "mp"), P("dp", "mp")),
        check_vma=False,
    )
```

```python
import functools
import math

import jax
import jax.numpy as jnp
from jax import lax
from jax.experimental import pallas as pl
from jax.experimental.pallas import tpu as pltpu
from jax.sharding import PartitionSpec as P

SOFTMAX_TEMPER = 0.02
EPSILON = 1e-06
MESH = pl.DeviceIdType.MESH
F32, BF16 = jnp.float32, jnp.bfloat16
SLOTS = 3
NY = NZ = 8
NX = 4
Q = 24
LISTED = 8
CHIP = 2 * Q
RANK = 16
ROWS = 384
WIDTH = 1024
HALF = WIDTH // 2
DEVS = 2 * NY * NZ
GROUP = NZ * CHIP
VOFF = SLOTS * Q
G_LANE, LOSS_LANE = 120, 121
TINY = 2.0**-80
NEG = -1e38


def nn(a, b):
    return lax.dot_general(a, b, (((1,), (0,)), ((), ())), preferred_element_type=F32)


def nt(a, b):
    return lax.dot_general(a, b, (((1,), (1,)), ((), ())), preferred_element_type=F32)


def tn(a, b):
    return lax.dot_general(a, b, (((0,), (0,)), ((), ())), preferred_element_type=F32)


def exact(dims, a, b):
    return lax.dot_general(a, b, (dims, ((), ())), preferred_element_type=F32, precision=lax.Precision.HIGHEST)


def split(x, parts):
    out = []
    for _ in range(parts):
        top = x.astype(BF16)
        out.append(top)
        x = x - top.astype(F32)
    return out


def iota(shape, dim):
    return lax.broadcasted_iota(jnp.int32, shape, dim)


def kernel(
    ids_ref, hidden_ref, down_ref, up_ref, pass_hbm, storage_hbm,
    loss_ref, pieces_ref, table_hbm,
    hbuf, mine, theirs, xb1, xb2, locs, lists, pick, picked, folds, diag, rsx, part, summed, got, back, wrec,
    cand, piece_out, piece_in, piece_sum, final, mixed_ref, pass_ref, storage_ref, table_ref,
    st_sem, e1_sem, e2_sem, l_sem, lz_sem, ly_sem, line_sem, ring_sem, sib_sem, rsx_sem, got_sem, w_sem, rs_sem, ag_sem,
    send_sem, small_sem, load_sem,
):
    me, mp = lax.axis_index("dp"), lax.axis_index("mp")
    core, chip_me = lax.rem(me, 2), me // 2
    y, z = chip_me // NZ, lax.rem(chip_me, NZ)

    def dev(yy, zz, c):
        return ((lax.rem(yy + NY, NY) * NZ + lax.rem(zz + NZ, NZ)) * 2 + c, mp)

    def push(src, dst, ssem, rsem, target):
        pltpu.make_async_remote_copy(
            src_ref=src, dst_ref=dst, send_sem=ssem, recv_sem=rsem, device_id=target, device_id_type=MESH
        ).start()

    def take(ref, sem):
        pltpu.make_async_copy(ref, ref, sem).wait()

    sibling = (chip_me * 2 + 1 - core, mp)

    sa, sb = NZ - (NZ - 1) * core, 1 + (NZ - 1) * core
    a = jnp.where(core == 0, y, z)
    b = jnp.where(core == 0, z, y)

    def line_dev(o):
        return (lax.rem(a + o + NY, NY) * sa + b * sb) * 2 + core

    def cross_dev(o):
        return (a * sa + lax.rem(b + o + NY, NY) * sb) * 2 + core

    loads = [
        pltpu.make_async_copy(storage_hbm, storage_ref, load_sem.at[0]),
        pltpu.make_async_copy(pass_hbm, pass_ref, load_sem.at[1]),
    ]
    for cp in loads:
        cp.start()

    bar = pltpu.get_barrier_semaphore()
    for o in (4, 3, 5, 2, 6, 1, 7):
        pl.semaphore_signal(bar, inc=1, device_id=(line_dev(o), mp), device_id_type=MESH)
        pl.semaphore_signal(bar, inc=1, device_id=(cross_dev(o), mp), device_id_type=MESH)
    pl.semaphore_signal(bar, inc=1, device_id=sibling, device_id_type=MESH)
    for i in range(1, NX):
        pl.semaphore_signal(bar, inc=1, device_id=(me, lax.rem(mp + i, NX)), device_id_type=MESH)

    hid32 = hidden_ref[...].astype(F32)
    mine[...] = jnp.concatenate([hid32, jnp.zeros((8, WIDTH), F32)], axis=0).astype(BF16)
    pl.semaphore_wait(bar, NY - 1 + NZ - 1 + 1 + NX - 1)
    push(mine, theirs, small_sem.at[0], st_sem, sibling)

    up32 = up_ref[...].astype(F32)
    left = jnp.concatenate([hid32, up32], axis=0).astype(BF16)
    right = jnp.concatenate([down_ref[...].astype(F32), up32, jnp.zeros((96, WIDTH), F32)], axis=0).astype(BF16)
    prod = nt(left, right)

    take(theirs, st_sem)
    theirs32 = theirs[0:Q, :].astype(F32)
    both = jnp.where(core == 0, jnp.concatenate([hid32, theirs32], axis=0), jnp.concatenate([theirs32, hid32], axis=0))
    hbuf[y, z] = both.astype(BF16)

    far = sorted((o for o in range(-3, 5) if o), key=abs, reverse=True)

    def bundle(c, p, bb):
        lanes = pl.ds(c * HALF, HALF)
        if c == 0:
            return hbuf.at[pl.ds(2 * p, 2), bb, :, lanes]
        return hbuf.at[bb, pl.ds(2 * p, 2), :, lanes]

    def single(c, aa, bb):
        lanes = pl.ds(c * HALF, HALF)
        return hbuf.at[aa, bb, :, lanes] if c == 0 else hbuf.at[bb, aa, :, lanes]

    pair = a // 2
    pairs = [lax.rem(pair + o, 4) for o in (0, 1, 3, 2)]

    def line_start(c):
        r = single(c, a, b)
        for o in far:
            push(r, r, send_sem, line_sem.at[pair], (line_dev(o), mp))

    def line_done(c, k):
        p = pairs[k]
        if k == 0:
            r = single(c, 2 * pair + 1 - lax.rem(a, 2), b)
        else:
            r = bundle(c, p, b)
        take(r, line_sem.at[p])
        both_chips = bundle(c, p, b)
        for o in (1, -1):
            push(both_chips, both_chips, send_sem, ring_sem.at[p, b], (cross_dev(o), mp))
        push(r, r, send_sem, sib_sem.at[p, b], sibling)

    def ring_event(c, k, t):
        p = pairs[k]
        for d in (1, -1):
            last = 4 if (k % 2 == 0) == (d > 0) else 3
            if t > last:
                continue
            bb = lax.rem(b - d * t + 2 * NY, NY)
            r = bundle(c, p, bb)
            take(r, ring_sem.at[p, bb])
            if t < last:
                push(r, r, send_sem, ring_sem.at[p, bb], (cross_dev(d), mp))
            push(r, r, send_sem, sib_sem.at[p, bb], sibling)

    for c in (0, 1):
        @pl.when(core == c)
        def _():
            line_start(c)

    loads[1].wait()
    biggest = jnp.max(jnp.max(jnp.abs(pass_ref[...].astype(F32)), axis=0, keepdims=True), axis=1, keepdims=True)
    lane40, row40 = iota((40, 128), 1), iota((40, 128), 0)
    xb1[mp] = jnp.where((lane40 == 40) & (row40 == 0), biggest, prod)
    for i in range(1, NX):
        push(xb1.at[mp], xb1.at[mp], small_sem.at[1], e1_sem, (me, lax.rem(mp + i, NX)))

    loads[0].wait()
    lane1 = iota((1, 128), 1)
    for j in range(Q * LISTED):
        pid = ids_ref[j % LISTED, j // LISTED]
        row = storage_ref[pl.ds(pid // 128, 1), :]
        locs[pl.ds(j, 1), :] = jnp.where(lane1 == lax.rem(pid, 128), row, 0).astype(F32)
    located = jnp.sum(locs[...], axis=1, keepdims=True)
    located = jnp.concatenate([located, jnp.full((64, 1), 1e6, F32)], axis=0)
    r256, l256 = iota((256, 256), 0), iota((256, 256), 1)
    as_row = jnp.sum(jnp.where(r256 == l256, located, 0.0), axis=0, keepdims=True)
    lists[0, pl.ds(me, 1), :] = as_row[:, 0:128]
    lists[1, pl.ds(me, 1), :] = as_row[:, 128:256]
    push(lists.at[:, pl.ds(me, 1), :], lists.at[:, pl.ds(me, 1), :], small_sem.at[2], l_sem, sibling)

    take(lists.at[:, pl.ds(0, 1), :], l_sem)

    def some_lists(first, n):
        return lists.at[:, pl.ds(pl.multiple_of(first, 2), n), :]

    for o in (4, 3, 5, 2, 6, 1, 7):
        r = some_lists(chip_me * 2, 2)
        push(r, r, small_sem.at[4], lz_sem.at[z], dev(y, z + o, core))

    def lists_on():
        def each(i, c):
            zz = lax.rem(z + i, NZ)
            take(some_lists((y * NZ + zz) * 2, 2), lz_sem.at[zz])
            return c
        lax.fori_loop(1, NZ, each, 0)
        for o in (4, 3, 5, 2, 6, 1, 7):
            r = some_lists(y * 2 * NZ, 2 * NZ)
            push(r, r, small_sem.at[5], ly_sem.at[y], dev(y + o, z, core))

    def lists_done():
        def each(i, c):
            yy = lax.rem(y + i, NY)
            take(some_lists(yy * 2 * NZ, 2 * NZ), ly_sem.at[yy])
            return c
        lax.fori_loop(1, NY, each, 0)

    def ring(first, last):
        for c in (0, 1):
            @pl.when(core == c)
            def _():
                for n in range(first, last):
                    if n < 4:
                        line_done(c, n)
                    else:
                        ring_event(c, n % 4, n // 4)

    ring(0, 6)

    take(xb1.at[pl.ds(0, NX - 1)], e1_sem)
    tot = xb1[0] + xb1[1] + xb1[2] + xb1[3]
    most = jnp.maximum(jnp.maximum(xb1[0], xb1[1]), jnp.maximum(xb1[2], xb1[3]))
    most = jnp.max(jnp.where((lane40 == 40) & (row40 == 0), most, 0.0))
    shrink = jnp.where(most > 2.0**40, TINY, 1.0)
    low_half = tot[0:Q, 0:RANK].astype(BF16)
    rolled = pltpu.roll(tot, 128 - RANK, 1)
    hid_up, gram = rolled[0:Q, 0:RANK], rolled[Q : Q + RANK, 0:RANK]
    mixed = hid32 + nn(low_half, up_ref[...])
    mixed_ref[...] = mixed
    xb2[mp] = jnp.broadcast_to(jnp.sum(mixed * mixed, axis=1, keepdims=True), (Q, 128))
    for i in range(1, NX):
        push(xb2.at[mp], xb2.at[mp], small_sem.at[3], e2_sem, (me, lax.rem(mp + i, NX)))

    ring(6, 8)
    lists_on()
    ring(8, 14)

    take(xb2.at[pl.ds(0, NX - 1)], e2_sem)
    inv_norm = lax.rsqrt((xb2[0] + xb2[1] + xb2[2] + xb2[3]) / (WIDTH * NX) + EPSILON)

    ring(14, 16)
    lists_done()

    wanted = jnp.concatenate([lists[0], lists[1]], axis=1) - (me * ROWS).astype(F32)
    here = (wanted >= 0.0) & (wanted < ROWS)
    earlier = nn(here.astype(F32).astype(BF16), (r256 < l256).astype(F32).astype(BF16))
    rows_iota = iota((DEVS, ROWS), 1).astype(F32)
    part_pu = jnp.zeros((DEVS, 128), F32)
    for s in range(SLOTS):
        col = jnp.sum(jnp.where(here & (earlier == s), wanted + 1.0, 0.0), axis=1, keepdims=True) - 1.0
        pk = (rows_iota == col).astype(F32).astype(BF16)
        pick[s] = pk
        picked[s] = (nn(pk, pass_ref[...]) * shrink).astype(BF16)
        f_lane = iota((GROUP, 128), 1) - s * Q
        folds[s] = ((f_lane == lax.rem(iota((GROUP, 128), 0), Q)) & (f_lane >= 0)).astype(F32).astype(BF16)
        up_at = jnp.concatenate(
            [jnp.zeros((VOFF + s * RANK, WIDTH), F32), up32, jnp.zeros((128 - VOFF - (s + 1) * RANK, WIDTH), F32)], axis=0
        ).astype(BF16)
        part_pu = part_pu + nt(picked[s], up_at)

    owner = jnp.floor((located + 0.5) * (1.0 / ROWS))
    hold = (iota((256, 128), 1).astype(F32) == owner).astype(F32)
    hold_b = hold.astype(BF16)
    rank = jnp.sum(hold * nn((r256 > l256).astype(F32).astype(BF16), hold_b), axis=1, keepdims=True)
    count = tn(hold_b, jnp.ones((256, 128), BF16))
    l_col = iota((256, 128), 1)
    pos_at = (iota((256, 128), 0) == LISTED * lax.rem(l_col, Q)) & (rank == (l_col // Q).astype(F32)) & (l_col < VOFF)
    positive = tn(hold_b, pos_at.astype(F32).astype(BF16))
    lane = iota((DEVS, 128), 1)
    valid = (count > (lane // Q).astype(F32)) & (lane < VOFF)

    row128 = iota((128, RANK), 0)
    at_rank = ((row128 >= VOFF) & (row128 < VOFF + SLOTS * RANK) & (lax.rem(row128 - VOFF + 128 * RANK, RANK) == iota((128, RANK), 1)))
    at_rank = at_rank.astype(F32)
    at_query = ((iota((Q, 128), 1) < VOFF) & (lax.rem(iota((Q, 128), 1), Q) == iota((Q, 128), 0))).astype(F32)
    spread = nn(nt(at_rank.astype(BF16), low_half).astype(BF16), at_query.astype(BF16))
    row_a, lane_a = iota((128, 128), 0), iota((128, 128), 1)
    same_slot = ((row_a + 128 * RANK - VOFF) // RANK - 128) == lane_a // Q
    spread = jnp.where(same_slot, spread, 0.0).astype(BF16)
    inv_lane = jnp.sum(inv_norm * at_query, axis=0, keepdims=True)

    ring(16, 20)

    def rest(c):
        for p in range(4):
            def each(bb, carry, p=p):
                both_chips = bundle(c, p, bb)
                at_home = bb == a

                @pl.when(at_home & (b // 2 == p))
                def _():
                    take(single(c, 2 * p, bb), sib_sem.at[p, bb])

                @pl.when(jnp.logical_not(at_home & (b // 2 == p)))
                def _():
                    take(both_chips, sib_sem.at[p, bb])
                return carry
            lax.fori_loop(0, NY, each, 0)

    for c in (0, 1):
        @pl.when(core == c)
        def _():
            rest(1 - c)

    lane48 = lax.rem(iota((Q, SLOTS * 16), 1), 16)

    def score(g, c):
        rows = pl.ds(pl.multiple_of(g * 16, 16), 16)
        s_g = jnp.concatenate([picked[s, rows, :] for s in range(SLOTS)], axis=0)
        d = nt(hbuf[g].reshape(GROUP, WIDTH), s_g)
        e = jnp.zeros((Q, SLOTS * 16), F32)
        for r in range(16):
            e = e + jnp.where(lane48 == r, d[r * Q : (r + 1) * Q, :], 0.0)
        e = jnp.concatenate([e, jnp.zeros((Q, 128 - SLOTS * 16), F32)], axis=1)
        e = jnp.transpose(jnp.concatenate([e, jnp.zeros((128 - Q, 128), F32)], axis=0))
        part[rows, :] = e[0:16, :] + pltpu.roll(e[16:32, :], Q, 1) + pltpu.roll(e[32:48, :], 2 * Q, 1)
        return c

    lax.fori_loop(0, NY, score, 0, unroll=True)
    part[...] = part[...] + part_pu + jnp.where(lane == G_LANE, shrink * (1.0 / NX), 0.0)

    quarter = DEVS // NX

    def q_rows(k):
        return part.at[pl.ds(pl.multiple_of(k * quarter, quarter), quarter), :]

    for i in range(1, NX):
        k = lax.rem(mp + i, NX)
        push(q_rows(k), rsx.at[mp], small_sem.at[6], rsx_sem, (me, k))
    rsx[mp] = part[pl.ds(pl.multiple_of(mp * quarter, quarter), quarter), :]
    take(rsx.at[pl.ds(0, NX - 1)], rsx_sem)
    summed[...] = rsx[0] + rsx[1] + rsx[2] + rsx[3]

    def swing(m):
        return ((8 - m) // 2) * (2 * lax.rem(m, 2) - 1)

    def far_first(m):
        return ((8 - m) // 2) * (1 if m % 2 else -1)

    def to_all(send):
        inner = [lax.rem(z + far_first(n) + NZ, NZ) * 2 + c for n in range(NZ) for c in (1 - core, core)]

        def far_rows(m, carry):
            base = lax.rem(y + swing(m) + NY, NY) * (2 * NZ)
            for n in inner:
                send(base + n)
            return carry

        lax.fori_loop(0, NY - 1, far_rows, 0)
        for n in inner[:-1]:
            send(y * (2 * NZ) + n)

    home = (me // quarter) == mp

    others = [lax.rem(mp + dk, NX) for dk in (2, 1, 3)]

    def give(m, c):
        first = lax.rem(z + swing(m) + NZ, NZ) * 2
        for j in (first, first + 1, first + 2 * NZ, first + 2 * NZ + 1):
            block = mp * quarter + j
            src = summed.at[pl.ds(j, 1), :]
            for k in others:
                push(src, got.at[pl.ds(me, 1), :], small_sem.at[7], got_sem, (block, k))

            @pl.when(block != me)
            def _():
                push(src, got.at[pl.ds(me, 1), :], small_sem.at[7], got_sem, (block, mp))
        return c

    lax.fori_loop(0, NZ, give, 0)

    @pl.when(home)
    def _():
        pltpu.make_async_copy(summed.at[pl.ds(lax.rem(me, quarter), 1), :], got.at[pl.ds(me, 1), :], got_sem).start()

    take(got, got_sem)

    g = got[...]
    unshrink = jnp.sum(jnp.where(lane == G_LANE, g, 0.0), axis=1, keepdims=True)
    unshrink = jnp.where(unshrink < 0.5, 1.0 / TINY, 1.0)
    ranks = jnp.where((lane >= VOFF) & (lane < VOFF + SLOTS * RANK), g, 0.0)
    raw = g
    for piece in split(ranks, 3):
        raw = raw + nn(piece, spread)
    raw = jnp.where(valid & (inv_lane > 0.0), raw * inv_lane * unshrink, 0.0)
    scale = 1.0 / (SOFTMAX_TEMPER * math.sqrt(WIDTH * NX))
    scores = jnp.where(valid, raw * scale, NEG)

    def over_slots(x, op, fill):
        x0 = op(op(x, pltpu.roll(x, 128 - Q, 1)), pltpu.roll(x, 128 - 2 * Q, 1))
        return jnp.where(lane1 < Q, x0, jnp.where(lane1 < 2 * Q, pltpu.roll(x0, Q, 1), jnp.where(lane1 < 3 * Q, pltpu.roll(x0, 2 * Q, 1), fill)))

    top = over_slots(jnp.max(scores, axis=0, keepdims=True), jnp.maximum, 0.0)
    expo = jnp.where(valid, jnp.exp(scores - top), 0.0)
    total = over_slots(jnp.sum(expo, axis=0, keepdims=True), jnp.add, 1.0)
    own = over_slots(jnp.sum(jnp.where(positive > 0.5, scores, 0.0), axis=0, keepdims=True), jnp.add, 0.0)
    loss = jnp.sum(jnp.where(lane1 < Q, jnp.log(total) + top - own, 0.0), axis=1, keepdims=True)
    weights = jnp.where(valid, (expo / total - positive) * scale, 0.0)
    tangent = over_slots(jnp.sum(weights * raw, axis=0, keepdims=True), jnp.add, 0.0) / (WIDTH * NX)
    w2 = weights * inv_lane
    v = jnp.zeros((DEVS, 128), F32)
    for piece in split(w2, 3):
        v = v + nt(piece, spread)
    back[...] = w2 + v + jnp.where(lane == LOSS_LANE, loss, 0.0)

    to_all(lambda t: push(back.at[pl.ds(t, 1), :], wrec.at[pl.ds(me, 1), :], small_sem.at[8], w_sem, (t, mp)))
    pltpu.make_async_copy(back.at[pl.ds(me, 1), :], wrec.at[pl.ds(me, 1), :], w_sem).start()

    z_all = exact(((0,), (0,)), weights, ranks * unshrink)
    z_all = jnp.where(lane_a >= VOFF, z_all, 0.0)
    same_t = ((lane_a + 128 * RANK - VOFF) // RANK - 128) == row_a // Q
    z_all = jnp.where(same_t, z_all, 0.0)
    w_pu = exact(((1,), (0,)), exact(((1,), (0,)), at_query, z_all), at_rank)
    inv_col = inv_norm[:, 0:1]
    q_up = inv_col * (hid_up + exact(((1,), (0,)), low_half.astype(F32), gram))
    tan_col = jnp.sum(jnp.where((iota((Q, 128), 1) < Q), at_query, 0.0) * tangent, axis=1, keepdims=True)
    low_grad = (inv_col * (w_pu - tan_col * q_up)).astype(BF16)
    ga = tn(low_grad, hidden_ref[...])
    pulled = (mixed_ref[...] * (inv_col * inv_col * tan_col)).astype(BF16)
    gb = -tn(low_half, pulled)

    take(wrec, w_sem)
    w = wrec[...]
    loss_ref[...] = jnp.sum(jnp.sum(jnp.where(lane == LOSS_LANE, w, 0.0), axis=0, keepdims=True), axis=1, keepdims=True) / (DEVS * Q)
    w_t = jnp.transpose(w)
    for s in range(SLOTS):
        for piece in split(w_t[VOFF + s * RANK : VOFF + (s + 1) * RANK, :], 2):
            gb = gb + nn(piece, picked[s]) * (1.0 / shrink)
    for j in range(WIDTH // 128):
        piece_out[0, pl.ds(j * RANK, RANK), :] = ga[:, j * 128 : (j + 1) * 128]
        piece_out[1, pl.ds(j * RANK, RANK), :] = gb[:, j * 128 : (j + 1) * 128]

    to_all(lambda t: push(piece_out.at[:, pl.ds(t, 1), :], piece_in.at[:, pl.ds(me, 1), :], small_sem.at[9], rs_sem, (t, mp)))
    pltpu.make_async_copy(piece_out.at[:, pl.ds(me, 1), :], piece_in.at[:, pl.ds(me, 1), :], rs_sem).start()

    hi, lo = split(w, 2)
    wide = (iota((DEVS, GROUP), 1) // Q) == lax.rem(iota((DEVS, GROUP), 0), 16)
    for s in range(SLOTS):
        diag[0, s] = jnp.where(wide, nt(hi, folds[s]), 0.0).astype(BF16)
        diag[1, s] = jnp.where(wide, nt(lo, folds[s]), 0.0).astype(BF16)

    def candidates(g_, c):
        rows = pl.ds(pl.multiple_of(g_ * 16, 16), 16)
        d = jnp.concatenate([diag[h, s, rows, :] for h in (0, 1) for s in range(SLOTS)], axis=0)
        o = nn(d, hbuf[g_].reshape(GROUP, WIDTH))
        o = o[0:48, :] + o[48:96, :]
        for s in range(SLOTS):
            cand[s, rows, :] = o[s * 16 : (s + 1) * 16, :]
        return c

    lax.fori_loop(0, NY, candidates, 0)
    table = jnp.zeros((ROWS, WIDTH), F32)
    for s in range(SLOTS):
        up_at = jnp.concatenate(
            [jnp.zeros((VOFF + s * RANK, WIDTH), F32), up32, jnp.zeros((128 - VOFF - (s + 1) * RANK, WIDTH), F32)], axis=0
        ).astype(BF16)
        cg = (cand[s] + nn(hi, up_at) + nn(lo, up_at)).astype(BF16)
        table = table + tn(pick[s], cg)
    table_ref[...] = table.astype(BF16)
    table_out = pltpu.make_async_copy(table_ref, table_hbm, load_sem.at[2])
    table_out.start()

    take(piece_in, rs_sem)
    piece_sum[...] = jnp.sum(piece_in[...], axis=1, keepdims=True)
    final[:, pl.ds(me, 1), :] = piece_sum[...]

    to_all(lambda t: push(piece_sum, final.at[:, pl.ds(me, 1), :], small_sem.at[10], ag_sem, (t, mp)))
    take(final.at[:, pl.ds(0, DEVS - 1), :], ag_sem)
    pieces_ref[...] = final[...]
    table_out.wait()

    half = pl.ds(0, HALF)
    take(hbuf.at[0, pl.ds(0, 7), :, half], send_sem)
    take(hbuf.at[pl.ds(0, 7), :, :, half], send_sem)
    take(hbuf.at[0, pl.ds(0, 7), :, half], send_sem)
    take(hbuf.at[pl.ds(0, 7), :, :, half], send_sem)
    take(mine, small_sem.at[0])
    take(xb1.at[pl.ds(0, NX - 1)], small_sem.at[1])
    take(lists.at[:, pl.ds(0, 1), :], small_sem.at[2])
    take(xb2.at[pl.ds(0, NX - 1)], small_sem.at[3])
    take(lists.at[:, pl.ds(0, 2 * 7), :], small_sem.at[4])
    take(lists.at[:, pl.ds(0, 2 * NZ * 7), :], small_sem.at[5])
    take(rsx.at[pl.ds(0, NX - 1)], small_sem.at[6])
    @pl.when(home)
    def _():
        take(got.at[pl.ds(0, DEVS - 1), :], small_sem.at[7])

    @pl.when(jnp.logical_not(home))
    def _():
        take(got, small_sem.at[7])

    take(wrec.at[pl.ds(0, DEVS - 1), :], small_sem.at[8])
    take(piece_in.at[:, pl.ds(0, DEVS - 1), :], small_sem.at[9])
    take(final.at[:, pl.ds(0, DEVS - 1), :], small_sem.at[10])


def finish(loss_in, pieces_ref, table_in, loss_ref, ga_ref, gb_ref, table_out):
    table_out[...] = table_in[...]
    loss_ref[...] = loss_in[...]
    for j in range(WIDTH // 128):
        ga_ref[:, pl.ds(j * 128, 128)] = pieces_ref[0, pl.ds(j * RANK, RANK), :]
        gb_ref[:, pl.ds(j * 128, 128)] = pieces_ref[1, pl.ds(j * RANK, RANK), :]


def shards(hidden, down, up, passages, ids, storage):
    vm, hbm = pl.BlockSpec(memory_space=pltpu.VMEM), pl.BlockSpec(memory_space=pl.ANY)
    dma = pltpu.SemaphoreType.DMA
    shape = jax.ShapeDtypeStruct
    loss, pieces, table = pl.pallas_call(
        kernel,
        out_shape=(shape((1, 1), F32), shape((2, DEVS, 128), F32), shape((ROWS, WIDTH), BF16)),
        in_specs=[pl.BlockSpec(memory_space=pltpu.SMEM), vm, vm, vm, hbm, hbm],
        out_specs=(vm, vm, hbm),
        scratch_shapes=[
            pltpu.VMEM((NY, NZ, CHIP, WIDTH), BF16),
            pltpu.VMEM((32, WIDTH), BF16),
            pltpu.VMEM((32, WIDTH), BF16),
            pltpu.VMEM((NX, 40, 128), F32),
            pltpu.VMEM((NX, Q, 128), F32),
            pltpu.VMEM((Q * LISTED, 128), F32),
            pltpu.VMEM((2, DEVS, 128), F32),
            pltpu.VMEM((SLOTS, DEVS, ROWS), BF16),
            pltpu.VMEM((SLOTS, DEVS, WIDTH), BF16),
            pltpu.VMEM((SLOTS, GROUP, 128), BF16),
            pltpu.VMEM((2, SLOTS, DEVS, GROUP), BF16),
            pltpu.VMEM((NX, DEVS // NX, 128), F32),
            pltpu.VMEM((DEVS, 128), F32),
            pltpu.VMEM((DEVS // NX, 128), F32),
            pltpu.VMEM((DEVS, 128), F32),
            pltpu.VMEM((DEVS, 128), F32),
            pltpu.VMEM((DEVS, 128), F32),
            pltpu.VMEM((SLOTS, DEVS, WIDTH), F32),
            pltpu.VMEM((2, DEVS, 128), F32),
            pltpu.VMEM((2, DEVS, 128), F32),
            pltpu.VMEM((2, 1, 128), F32),
            pltpu.VMEM((2, DEVS, 128), F32),
            pltpu.VMEM((Q, WIDTH), F32),
            pltpu.VMEM((ROWS, WIDTH), BF16),
            pltpu.VMEM((ROWS, 128), jnp.int32),
            pltpu.VMEM((ROWS, WIDTH), BF16),
            dma, dma, dma, dma,
            dma((NZ,)), dma((NY,)),
            dma((4,)), dma((4, NY)), dma((4, NY)),
            dma, dma, dma, dma, dma,
            dma, dma((11,)), dma((3,)),
        ],
        compiler_params=pltpu.CompilerParams(collective_id=0, has_side_effects=True, vmem_limit_bytes=56 << 20),
        name="contrastive",
    )(ids.T, hidden, down, up, passages, storage.reshape(ROWS, 128))
    loss, ga, gb, table = pl.pallas_call(
        finish,
        out_shape=(shape((1, 1), F32), shape((RANK, WIDTH), F32), shape((RANK, WIDTH), F32), shape((ROWS, WIDTH), BF16)),
        in_specs=[vm, vm, vm],
        out_specs=(vm, vm, vm, vm),
        name="finish",
    )(loss, pieces, table)
    return loss.reshape(()), ga, gb, table


def solution(mesh):
    return jax.shard_map(
        shards,
        mesh=mesh,
        in_specs=(P("dp", "mp"), P(None, "mp"), P(None, "mp"), P("dp", "mp"), P("dp", None), P()),
        out_specs=(P(), P(None, "mp"), P(None, "mp"), P("dp", "mp")),
        check_vma=False,
    )
```

```python
import functools
import math

import jax
import jax.numpy as jnp
from jax import lax
from jax.experimental import pallas as pl
from jax.experimental.pallas import tpu as pltpu
from jax.sharding import PartitionSpec as P

SOFTMAX_TEMPER = 0.02
EPSILON = 1e-06
MESH = pl.DeviceIdType.MESH
F32, BF16 = jnp.float32, jnp.bfloat16
SLOTS = 3
NY = NZ = 8
NX = 4
Q = 24
LISTED = 8
RANK = 16
ROWS = 384
WIDTH = 1024
HALF = WIDTH // 2
TALL, SHORT = 16, 8
DEVS = 2 * NY * NZ
CHIPS = NY * NZ
GROUP = 16 * TALL
VOFF = SLOTS * Q
G_LANE, LOSS_LANE = 120, 121
TINY = 2.0**-80
NEG = -1e38


def nn(a, b):
    return lax.dot_general(a, b, (((1,), (0,)), ((), ())), preferred_element_type=F32)


def nt(a, b):
    return lax.dot_general(a, b, (((1,), (1,)), ((), ())), preferred_element_type=F32)


def tn(a, b):
    return lax.dot_general(a, b, (((0,), (0,)), ((), ())), preferred_element_type=F32)


def exact(dims, a, b):
    return lax.dot_general(a, b, (dims, ((), ())), preferred_element_type=F32, precision=lax.Precision.HIGHEST)


def split(x, parts):
    out = []
    for _ in range(parts):
        top = x.astype(BF16)
        out.append(top)
        x = x - top.astype(F32)
    return out


def iota(shape, dim):
    return lax.broadcasted_iota(jnp.int32, shape, dim)


def kernel(
    ids_hbm, hidden_hbm, down_hbm, up_hbm, pass_hbm, storage_hbm,
    loss_ref, pieces_ref, table_hbm,
    ids_ref, hidden_ref, down_ref, up_ref, hbuf, xb1, xb2, locs, lists, pick, picked, slots, flags, losses, folds, diag, rsx, part, summed, got, back, wrec,
    cand, cand_out, cand_all, piece_out, piece_in, piece_sum, final, mixed_ref, pass_ref, storage_ref, table_ref,
    e1_sem, e2_sem, l_sem, lz_sem, ly_sem, ring_sem, guest_sem, flag_sem, cand_sem, loss_sem, rsx_sem, got_sem, w_sem, rs_sem, ag_sem,
    send_sem, small_sem, load_sem,
):
    me, mp = lax.axis_index("dp"), lax.axis_index("mp")
    core, chip_me = lax.rem(me, 2), me // 2
    y, z = chip_me // NZ, lax.rem(chip_me, NZ)

    def dev(yy, zz, c):
        return ((lax.rem(yy + NY, NY) * NZ + lax.rem(zz + NZ, NZ)) * 2 + c, mp)

    def push(src, dst, ssem, rsem, target):
        pltpu.make_async_remote_copy(
            src_ref=src, dst_ref=dst, send_sem=ssem, recv_sem=rsem, device_id=target, device_id_type=MESH
        ).start()

    def take(ref, sem):
        pltpu.make_async_copy(ref, ref, sem).wait()

    sibling = (chip_me * 2 + 1 - core, mp)

    sa, sb = NZ - (NZ - 1) * core, 1 + (NZ - 1) * core
    a = jnp.where(core == 0, y, z)
    b = jnp.where(core == 0, z, y)

    def line_dev(o):
        return (lax.rem(a + o + NY, NY) * sa + b * sb) * 2 + core

    def cross_dev(o):
        return (a * sa + lax.rem(b + o + NY, NY) * sb) * 2 + core

    loads = [
        pltpu.make_async_copy(src, dst, load_sem.at[i])
        for i, (src, dst) in enumerate((
            (hidden_hbm, hidden_ref), (up_hbm, up_ref), (down_hbm, down_ref),
            (pass_hbm, pass_ref), (storage_hbm, storage_ref), (ids_hbm, ids_ref),
        ))
    ]
    loads[0].start()

    bar = pltpu.get_barrier_semaphore()
    for o in (4, 3, 5, 2, 6, 1, 7):
        pl.semaphore_signal(bar, inc=1, device_id=(line_dev(o), mp), device_id_type=MESH)
        pl.semaphore_signal(bar, inc=1, device_id=(cross_dev(o), mp), device_id_type=MESH)
    pl.semaphore_signal(bar, inc=1, device_id=sibling, device_id_type=MESH)
    for i in range(1, NX):
        pl.semaphore_signal(bar, inc=1, device_id=(me, lax.rem(mp + i, NX)), device_id_type=MESH)

    for cp in loads[1:]:
        cp.start()
    loads[0].wait()
    hid32 = hidden_ref[...].astype(F32)
    hbuf[chip_me, :, 0:WIDTH] = hid32[0:TALL].astype(BF16)
    folded = jnp.concatenate([hid32[TALL:Q, 0:HALF], hid32[TALL:Q, HALF:WIDTH]], axis=0)
    hbuf[chip_me, :, WIDTH : WIDTH + HALF] = folded.astype(BF16)
    pl.semaphore_wait(bar, NY - 1 + NZ - 1 + 1 + NX - 1)

    def chip_of(aa, bb):
        return lax.rem(aa + 2 * NY, NY) * sa + lax.rem(bb + 2 * NY, NY) * sb

    def pass_on(ci, target):
        push(hbuf.at[ci], hbuf.at[ci], send_sem, ring_sem.at[ci], (target, mp))

    for o in (-1, 1, -2, 2, -3, 3, 4):
        pass_on(chip_me, line_dev(o))
    ahead, behind = cross_dev(1), cross_dev(-1)
    offsets = (0, 1, -1, 2, -2, 3, -3, 4)

    def event(t, k):
        if t == 0:
            ci = chip_of(a + offsets[k], b)
            if k > 0:
                take(hbuf.at[ci], ring_sem.at[ci])
            pass_on(ci, ahead)
            pass_on(ci, behind)
            return
        for d in (1, -1):
            last = 4 if (k % 2 == 0) == (d > 0) else 3
            if t <= last:
                ci = chip_of(a + offsets[k], b - d * t)
                take(hbuf.at[ci], ring_sem.at[ci])
                if t < last:
                    pass_on(ci, ahead if d > 0 else behind)

    events = sorted(((t, k) for t in range(5) for k in range(NY)), key=lambda e: (e[0] == 4, 4 * e[0] + e[1]))

    def ring(first, last):
        for t, k in events[first:last]:
            event(t, k)

    loads[1].wait()
    loads[2].wait()
    up32 = up_ref[...].astype(F32)
    left = jnp.concatenate([hid32, up32], axis=0).astype(BF16)
    right = jnp.concatenate([down_ref[...].astype(F32), up32, jnp.zeros((96, WIDTH), F32)], axis=0).astype(BF16)
    prod = nt(left, right)

    loads[3].wait()
    biggest = jnp.max(jnp.max(jnp.abs(pass_ref[...].astype(F32)), axis=0, keepdims=True), axis=1, keepdims=True)
    lane40, row40 = iota((40, 128), 1), iota((40, 128), 0)
    xb1[mp] = jnp.where((lane40 == 40) & (row40 == 0), biggest, prod)
    for i in range(1, NX):
        push(xb1.at[mp], xb1.at[mp], small_sem.at[1], e1_sem, (me, lax.rem(mp + i, NX)))

    loads[4].wait()
    loads[5].wait()
    lane1 = iota((1, 128), 1)
    for j in range(Q * LISTED):
        pid = ids_ref[j % LISTED, j // LISTED]
        row = storage_ref[pl.ds(pid // 128, 1), :]
        locs[pl.ds(j, 1), :] = jnp.where(lane1 == lax.rem(pid, 128), row, 0).astype(F32)
    located = jnp.sum(locs[...], axis=1, keepdims=True)
    located = jnp.concatenate([located, jnp.full((64, 1), 1e6, F32)], axis=0)
    r256, l256 = iota((256, 256), 0), iota((256, 256), 1)
    as_row = jnp.sum(jnp.where(r256 == l256, located, 0.0), axis=0, keepdims=True)
    lists[0, core, pl.ds(chip_me, 1), :] = as_row[:, 0:128]
    lists[1, core, pl.ds(chip_me, 1), :] = as_row[:, 128:256]
    own_list = lists.at[:, core, pl.ds(chip_me, 1), :]
    push(own_list, own_list, small_sem.at[2], l_sem, sibling)

    take(lists.at[:, 0, pl.ds(0, 1), :], l_sem)

    def some_lists(first, n):
        return lists.at[:, :, pl.ds(pl.multiple_of(first, n), n), :]

    for o in (4, 3, 5, 2, 6, 1, 7):
        r = some_lists(chip_me, 1)
        push(r, r, small_sem.at[4], lz_sem.at[z], dev(y, z + o, core))

    def lists_on():
        def each(i, c):
            zz = lax.rem(z + i, NZ)
            take(some_lists(y * NZ + zz, 1), lz_sem.at[zz])
            return c
        lax.fori_loop(1, NZ, each, 0)
        for o in (4, 3, 5, 2, 6, 1, 7):
            r = some_lists(y * NZ, NZ)
            push(r, r, small_sem.at[5], ly_sem.at[y], dev(y + o, z, core))

    def lists_done():
        def each(i, c):
            yy = lax.rem(y + i, NY)
            take(some_lists(yy * NZ, NZ), ly_sem.at[yy])
            return c
        lax.fori_loop(1, NY, each, 0)

    ring(0, 8)

    take(xb1.at[pl.ds(0, NX - 1)], e1_sem)
    tot = xb1[0] + xb1[1] + xb1[2] + xb1[3]
    most = jnp.maximum(jnp.maximum(xb1[0], xb1[1]), jnp.maximum(xb1[2], xb1[3]))
    most = jnp.max(jnp.where((lane40 == 40) & (row40 == 0), most, 0.0))
    shrink = jnp.where(most > 2.0**40, TINY, 1.0)
    low_half = tot[0:Q, 0:RANK].astype(BF16)
    rolled = pltpu.roll(tot, 128 - RANK, 1)
    hid_up, gram = rolled[0:Q, 0:RANK], rolled[Q : Q + RANK, 0:RANK]
    mixed = hid32 + nn(low_half, up_ref[...])
    mixed_ref[...] = mixed
    xb2[mp] = jnp.broadcast_to(jnp.sum(mixed * mixed, axis=1, keepdims=True), (Q, 128))
    for i in range(1, NX):
        push(xb2.at[mp], xb2.at[mp], small_sem.at[3], e2_sem, (me, lax.rem(mp + i, NX)))

    flags[core] = jnp.full((8, 128), shrink, F32)
    push(flags.at[core], flags.at[core], small_sem.at[11], flag_sem, sibling)

    ring(8, 14)
    lists_on()
    ring(14, 24)

    take(xb2.at[pl.ds(0, NX - 1)], e2_sem)
    inv_norm = lax.rsqrt((xb2[0] + xb2[1] + xb2[2] + xb2[3]) / (WIDTH * NX) + EPSILON)

    ring(24, 32)
    lists_done()

    wanted = jnp.concatenate([lists[0].reshape(DEVS, 128), lists[1].reshape(DEVS, 128)], axis=1) - (me * ROWS).astype(F32)
    here = (wanted >= 0.0) & (wanted < ROWS)
    earlier = nn(here.astype(F32).astype(BF16), (r256 < l256).astype(F32).astype(BF16))
    rows_iota = iota((DEVS, ROWS), 1).astype(F32)
    for s in range(SLOTS):
        col = jnp.sum(jnp.where(here & (earlier == s), wanted + 1.0, 0.0), axis=1, keepdims=True) - 1.0
        pk = (rows_iota == col).astype(F32).astype(BF16)
        pick[s] = pk
        picked[s] = (nn(pk, pass_ref[...]) * shrink).astype(BF16)
        f_lane = iota((GROUP, 128), 1) - s * Q
        f_row = iota((GROUP, 128), 0)
        folds[0, s] = (f_lane == lax.rem(f_row, TALL)).astype(F32).astype(BF16)
        folds[1, s] = (f_lane == TALL + lax.rem(f_row, SHORT)).astype(F32).astype(BF16)
    guests = pl.ds(pl.multiple_of((1 - core) * CHIPS, CHIPS), CHIPS)
    push(picked.at[:, guests, :], slots.at[core], small_sem.at[0], guest_sem, sibling)
    for s in range(SLOTS):
        slots[core, s] = picked[s, pl.ds(pl.multiple_of(core * CHIPS, CHIPS), CHIPS), :]

    owner = jnp.floor((located + 0.5) * (1.0 / ROWS))
    owner_chip = jnp.floor(owner * 0.5)
    owner = (owner - 2.0 * owner_chip) * CHIPS + owner_chip
    hold = (iota((256, 128), 1).astype(F32) == owner).astype(F32)
    hold_b = hold.astype(BF16)
    rank = jnp.sum(hold * nn((r256 > l256).astype(F32).astype(BF16), hold_b), axis=1, keepdims=True)
    count = tn(hold_b, jnp.ones((256, 128), BF16))
    l_col = iota((256, 128), 1)
    pos_at = (iota((256, 128), 0) == LISTED * lax.rem(l_col, Q)) & (rank == (l_col // Q).astype(F32)) & (l_col < VOFF)
    positive = tn(hold_b, pos_at.astype(F32).astype(BF16))
    lane = iota((DEVS, 128), 1)
    valid = (count > (lane // Q).astype(F32)) & (lane < VOFF)

    row128 = iota((128, RANK), 0)
    at_rank = ((row128 >= VOFF) & (row128 < VOFF + SLOTS * RANK) & (lax.rem(row128 - VOFF + 128 * RANK, RANK) == iota((128, RANK), 1)))
    at_rank = at_rank.astype(F32)
    at_query = ((iota((Q, 128), 1) < VOFF) & (lax.rem(iota((Q, 128), 1), Q) == iota((Q, 128), 0))).astype(F32)
    spread = nn(nt(at_rank.astype(BF16), low_half).astype(BF16), at_query.astype(BF16))
    row_a, lane_a = iota((128, 128), 0), iota((128, 128), 1)
    same_slot = ((row_a + 128 * RANK - VOFF) // RANK - 128) == lane_a // Q
    spread = jnp.where(same_slot, spread, 0.0).astype(BF16)
    inv_lane = jnp.sum(inv_norm * at_query, axis=0, keepdims=True)

    ring(32, 36)

    take(slots.at[0], guest_sem)
    take(flags.at[0], flag_sem)

    def slot_rows(s):
        return slots[:, s].reshape(DEVS, WIDTH)

    def up_lanes(s):
        return jnp.concatenate(
            [jnp.zeros((VOFF + s * RANK, WIDTH), F32), up32, jnp.zeros((128 - VOFF - (s + 1) * RANK, WIDTH), F32)], axis=0
        ).astype(BF16)

    part_pu = jnp.zeros((DEVS, 128), F32)
    for s in range(SLOTS):
        part_pu = part_pu + nt(slot_rows(s), up_lanes(s))

    ring(36, 40)

    SG = 2 * SLOTS * 16
    block_t = lax.rem(iota((TALL, SG), 1), 16)
    block_s = lax.rem(iota((SHORT, SG), 1), 16)

    def tall(g):
        return hbuf[pl.ds(g * 16, 16), :, 0:WIDTH].reshape(GROUP, WIDTH)

    def short(g):
        return hbuf[pl.ds(g * 16, 16), :, WIDTH : WIDTH + HALF].reshape(GROUP, HALF)

    for g in range(CHIPS // 16):
        rows = pl.ds(g * 16, 16)
        s_g = jnp.concatenate([slots[h, s, rows, :] for h in (0, 1) for s in range(SLOTS)], axis=0)
        d = nt(tall(g), s_g)
        d_lo, d_hi = nt(short(g), s_g[:, 0:HALF]), nt(short(g), s_g[:, HALF:WIDTH])
        e, f = jnp.zeros((TALL, SG), F32), jnp.zeros((SHORT, SG), F32)
        for r in range(16):
            at = r * TALL
            e = e + jnp.where(block_t == r, d[at : at + TALL, :], 0.0)
            f = f + jnp.where(block_s == r, d_lo[at : at + SHORT, :] + d_hi[at + SHORT : at + TALL, :], 0.0)
        e = jnp.concatenate([e, f], axis=0)
        e = jnp.concatenate([e, jnp.zeros((Q, 128 - SG), F32)], axis=1)
        e = jnp.transpose(jnp.concatenate([e, jnp.zeros((128 - Q, 128), F32)], axis=0))
        for h in (0, 1):
            at = h * SLOTS * 16
            one = e[at : at + 16, :] + pltpu.roll(e[at + 16 : at + 32, :], Q, 1) + pltpu.roll(e[at + 32 : at + 48, :], 2 * Q, 1)
            one = one + part_pu[h * CHIPS + g * 16 : h * CHIPS + (g + 1) * 16, :]
            part[h, rows, :] = one + jnp.where(lane[0:16] == G_LANE, flags[h, 0:1, :] * (1.0 / NX), 0.0)

    quarter = CHIPS // NX

    def q_rows(k):
        return part.at[:, pl.ds(pl.multiple_of(k * quarter, quarter), quarter), :]

    for i in range(1, NX):
        k = lax.rem(mp + i, NX)
        push(q_rows(k), rsx.at[mp], small_sem.at[6], rsx_sem, (me, k))
    rsx[mp] = part[:, pl.ds(pl.multiple_of(mp * quarter, quarter), quarter), :]
    take(rsx.at[pl.ds(0, NX - 1)], rsx_sem)
    summed[...] = rsx[0] + rsx[1] + rsx[2] + rsx[3]

    def swing(m):
        return ((8 - m) // 2) * (2 * lax.rem(m, 2) - 1)

    def far_first(m):
        return ((8 - m) // 2) * (1 if m % 2 else -1)

    def to_all(send, both):
        inner = [lax.rem(z + far_first(n) + NZ, NZ) for n in range(NZ)]
        cores = (1 - core, core) if both else (core,)

        def far_rows(m, carry):
            base = lax.rem(y + swing(m) + NY, NY) * NZ
            for n in inner:
                for c in cores:
                    send(base + n, c)
            return carry

        lax.fori_loop(0, NY - 1, far_rows, 0)
        for i, n in enumerate(inner):
            for c in cores[: len(cores) if i < NZ - 1 else len(cores) - 1]:
                send(y * NZ + n, c)

    def row_of(ref, chip):
        return ref.at[:, pl.ds(chip, 1), :]

    home = (chip_me // quarter) == mp
    others = [lax.rem(mp + dk, NX) for dk in (2, 1, 3)]

    def give(m, c):
        first = lax.rem(z + swing(m) + NZ, NZ)
        for j in (first, first + NZ):
            chip = mp * quarter + j
            for k in others:
                push(row_of(summed, j), row_of(got, chip_me), small_sem.at[7], got_sem, (chip * 2 + core, k))

            @pl.when(chip != chip_me)
            def _():
                push(row_of(summed, j), row_of(got, chip_me), small_sem.at[7], got_sem, (chip * 2 + core, mp))
        return c

    lax.fori_loop(0, NZ, give, 0)

    @pl.when(home)
    def _():
        pltpu.make_async_copy(row_of(summed, lax.rem(chip_me, quarter)), row_of(got, chip_me), got_sem).start()

    take(got, got_sem)

    g = got[...].reshape(DEVS, 128)
    unshrink = jnp.sum(jnp.where(lane == G_LANE, g, 0.0), axis=1, keepdims=True)
    unshrink = jnp.where(unshrink < 0.5, 1.0 / TINY, 1.0)
    ranks = jnp.where((lane >= VOFF) & (lane < VOFF + SLOTS * RANK), g, 0.0)
    raw = g
    for piece in split(ranks, 3):
        raw = raw + nn(piece, spread)
    raw = jnp.where(valid & (inv_lane > 0.0), raw * inv_lane * unshrink, 0.0)
    scale = 1.0 / (SOFTMAX_TEMPER * math.sqrt(WIDTH * NX))
    scores = jnp.where(valid, raw * scale, NEG)

    def over_slots(x, op, fill):
        x0 = op(op(x, pltpu.roll(x, 128 - Q, 1)), pltpu.roll(x, 128 - 2 * Q, 1))
        return jnp.where(lane1 < Q, x0, jnp.where(lane1 < 2 * Q, pltpu.roll(x0, Q, 1), jnp.where(lane1 < 3 * Q, pltpu.roll(x0, 2 * Q, 1), fill)))

    top = over_slots(jnp.max(scores, axis=0, keepdims=True), jnp.maximum, 0.0)
    expo = jnp.where(valid, jnp.exp(scores - top), 0.0)
    total = over_slots(jnp.sum(expo, axis=0, keepdims=True), jnp.add, 1.0)
    own = over_slots(jnp.sum(jnp.where(positive > 0.5, scores, 0.0), axis=0, keepdims=True), jnp.add, 0.0)
    loss = jnp.sum(jnp.where(lane1 < Q, jnp.log(total) + top - own, 0.0), axis=1, keepdims=True)
    weights = jnp.where(valid, (expo / total - positive) * scale, 0.0)
    tangent = over_slots(jnp.sum(weights * raw, axis=0, keepdims=True), jnp.add, 0.0) / (WIDTH * NX)
    w2 = weights * inv_lane
    v = jnp.zeros((DEVS, 128), F32)
    for piece in split(w2, 3):
        v = v + nt(piece, spread)
    back[...] = (w2 + v + jnp.where(lane == LOSS_LANE, loss, 0.0)).reshape(2, CHIPS, 128)

    to_all(lambda chip, c: push(row_of(back, chip), row_of(wrec, chip_me), small_sem.at[8], w_sem, (chip * 2 + c, mp)), False)
    pltpu.make_async_copy(row_of(back, chip_me), row_of(wrec, chip_me), w_sem).start()

    z_all = exact(((0,), (0,)), weights, ranks * unshrink)
    z_all = jnp.where(lane_a >= VOFF, z_all, 0.0)
    same_t = ((lane_a + 128 * RANK - VOFF) // RANK - 128) == row_a // Q
    z_all = jnp.where(same_t, z_all, 0.0)
    w_pu = exact(((1,), (0,)), exact(((1,), (0,)), at_query, z_all), at_rank)
    inv_col = inv_norm[:, 0:1]
    q_up = inv_col * (hid_up + exact(((1,), (0,)), low_half.astype(F32), gram))
    tan_col = jnp.sum(jnp.where((iota((Q, 128), 1) < Q), at_query, 0.0) * tangent, axis=1, keepdims=True)
    low_grad = (inv_col * (w_pu - tan_col * q_up)).astype(BF16)
    ga = tn(low_grad, hidden_ref[...])
    pulled = (mixed_ref[...] * (inv_col * inv_col * tan_col)).astype(BF16)
    gb = -tn(low_half, pulled)

    take(wrec, w_sem)
    w = wrec[...].reshape(DEVS, 128)
    lost = jnp.where((lane == LOSS_LANE) & (iota((DEVS, 128), 0) < CHIPS), w, 0.0)
    losses[core] = jnp.broadcast_to(jnp.sum(jnp.sum(lost, axis=0, keepdims=True), axis=1, keepdims=True), (8, 128))
    push(losses.at[core], losses.at[core], small_sem.at[13], loss_sem, sibling)
    w_t = jnp.transpose(w) * jnp.where(lane1 < CHIPS, 1.0 / flags[0, 0:1, :], 1.0 / flags[1, 0:1, :])
    for s in range(SLOTS):
        for piece in split(w_t[VOFF + s * RANK : VOFF + (s + 1) * RANK, :], 2):
            gb = gb + nn(piece, slot_rows(s))
    for j in range(WIDTH // 128):
        piece_out[0, pl.ds(j * RANK, RANK), :] = ga[:, j * 128 : (j + 1) * 128]
        piece_out[1, pl.ds(j * RANK, RANK), :] = gb[:, j * 128 : (j + 1) * 128]

    to_all(lambda chip, c: push(row_of(piece_out, chip * 2 + c), row_of(piece_in, me), small_sem.at[9], rs_sem, (chip * 2 + c, mp)), True)
    pltpu.make_async_copy(piece_out.at[:, pl.ds(me, 1), :], piece_in.at[:, pl.ds(me, 1), :], rs_sem).start()

    hi, lo = split(w, 2)
    d_lane = iota((DEVS, GROUP), 1)
    wide = (d_lane // TALL) == lax.rem(iota((DEVS, GROUP), 0), 16)
    first_half = lax.rem(d_lane // SHORT, 2) == 0
    for s in range(SLOTS):
        for i, piece in enumerate((hi, lo)):
            diag[0, i, s] = jnp.where(wide, nt(piece, folds[0, s]), 0.0).astype(BF16)
            low8 = jnp.where(wide, nt(piece, folds[1, s]), 0.0)
            diag[1, i, s] = jnp.where(first_half, low8, 0.0).astype(BF16)
            diag[2, i, s] = jnp.where(first_half, 0.0, low8).astype(BF16)

    def candidates(g_, c):
        rows = pl.ds(pl.multiple_of(g_ * 16, 16), 16)
        d0, d1, d2 = (
            jnp.concatenate(
                [diag[n, i, s, pl.ds(pl.multiple_of(h * CHIPS + g_ * 16, 16), 16), :] for i in (0, 1) for h in (0, 1) for s in range(SLOTS)],
                axis=0,
            )
            for n in range(3)
        )
        o = nn(d0, tall(g_)) + jnp.concatenate([nn(d1, short(g_)), nn(d2, short(g_))], axis=1)
        o = o[0:SG, :] + o[SG : 2 * SG, :]
        for h in (0, 1):
            for s in range(SLOTS):
                at = (h * SLOTS + s) * 16
                cand[h, s, rows, :] = o[at : at + 16, :]
        return c

    lax.fori_loop(0, CHIPS // 16, candidates, 0)
    for s in range(SLOTS):
        up_at = up_lanes(s)
        cg = cand[:, s].reshape(DEVS, WIDTH) + nn(hi, up_at) + nn(lo, up_at)
        cand_out[:, s] = cg.astype(BF16).reshape(2, CHIPS, WIDTH)
    push(cand_out.at[1 - core], cand_all.at[core], small_sem.at[12], cand_sem, sibling)
    cand_all[core] = cand_out[core]

    take(piece_in, rs_sem)
    piece_sum[...] = jnp.sum(piece_in[...], axis=1, keepdims=True)
    final[:, pl.ds(me, 1), :] = piece_sum[...]

    to_all(lambda chip, c: push(piece_sum, row_of(final, me), small_sem.at[10], ag_sem, (chip * 2 + c, mp)), True)
    take(cand_all.at[0], cand_sem)
    table = jnp.zeros((ROWS, WIDTH), F32)
    for s in range(SLOTS):
        table = table + tn(pick[s], cand_all[:, s].reshape(DEVS, WIDTH))
    table_ref[...] = table.astype(BF16)
    table_out = pltpu.make_async_copy(table_ref, table_hbm, load_sem.at[6])
    table_out.start()

    take(final.at[:, pl.ds(0, DEVS - 1), :], ag_sem)
    pieces_ref[...] = final[...]
    take(losses.at[0], loss_sem)
    loss_ref[...] = (losses[0, 0:1, 0:1] + losses[1, 0:1, 0:1]) / (DEVS * Q)
    table_out.wait()

    take(hbuf.at[pl.ds(0, CHIPS - 1)], send_sem)
    take(picked.at[:, pl.ds(0, CHIPS), :], small_sem.at[0])
    take(xb1.at[pl.ds(0, NX - 1)], small_sem.at[1])
    take(lists.at[:, 0, pl.ds(0, 1), :], small_sem.at[2])
    take(xb2.at[pl.ds(0, NX - 1)], small_sem.at[3])
    take(lists.at[:, :, pl.ds(0, NZ - 1), :], small_sem.at[4])
    take(lists.at[:, :, pl.ds(0, NZ * (NY - 1)), :], small_sem.at[5])
    take(rsx.at[pl.ds(0, NX - 1)], small_sem.at[6])
    @pl.when(home)
    def _():
        take(got.at[:, pl.ds(0, CHIPS - 1), :], small_sem.at[7])

    @pl.when(jnp.logical_not(home))
    def _():
        take(got, small_sem.at[7])

    take(wrec.at[:, pl.ds(0, CHIPS - 1), :], small_sem.at[8])
    take(piece_in.at[:, pl.ds(0, DEVS - 1), :], small_sem.at[9])
    take(final.at[:, pl.ds(0, DEVS - 1), :], small_sem.at[10])
    take(flags.at[0], small_sem.at[11])
    take(losses.at[0], small_sem.at[13])
    take(cand_out.at[0], small_sem.at[12])


def finish(loss_in, pieces_ref, table_in, loss_ref, ga_ref, gb_ref, table_out, buf, in_sem, out_sem):
    step = ROWS // 4
    ins = [
        pltpu.make_async_copy(table_in.at[pl.ds(i * step, step), :], buf.at[pl.ds(i * step, step), :], in_sem.at[i])
        for i in range(4)
    ]
    outs = [
        pltpu.make_async_copy(buf.at[pl.ds(i * step, step), :], table_out.at[pl.ds(i * step, step), :], out_sem.at[i])
        for i in range(4)
    ]
    for cp in ins:
        cp.start()
    loss_ref[...] = loss_in[...]
    for j in range(WIDTH // 128):
        ga_ref[:, pl.ds(j * 128, 128)] = pieces_ref[0, pl.ds(j * RANK, RANK), :]
        gb_ref[:, pl.ds(j * 128, 128)] = pieces_ref[1, pl.ds(j * RANK, RANK), :]
    for cin, cout in zip(ins, outs, strict=True):
        cin.wait()
        cout.start()
    for cp in outs:
        cp.wait()


def shards(hidden, down, up, passages, ids, storage):
    vm, hbm = pl.BlockSpec(memory_space=pltpu.VMEM), pl.BlockSpec(memory_space=pl.ANY)
    dma = pltpu.SemaphoreType.DMA
    shape = jax.ShapeDtypeStruct
    loss, pieces, table = pl.pallas_call(
        kernel,
        out_shape=(shape((1, 1), F32), shape((2, DEVS, 128), F32), shape((ROWS, WIDTH), BF16)),
        in_specs=[hbm] * 6,
        out_specs=(vm, vm, hbm),
        scratch_shapes=[
            pltpu.SMEM((LISTED, Q), jnp.int32),
            pltpu.VMEM((Q, WIDTH), BF16),
            pltpu.VMEM((RANK, WIDTH), BF16),
            pltpu.VMEM((RANK, WIDTH), BF16),
            pltpu.VMEM((CHIPS, TALL, WIDTH + HALF), BF16),
            pltpu.VMEM((NX, 40, 128), F32),
            pltpu.VMEM((NX, Q, 128), F32),
            pltpu.VMEM((Q * LISTED, 128), F32),
            pltpu.VMEM((2, 2, CHIPS, 128), F32),
            pltpu.VMEM((SLOTS, DEVS, ROWS), BF16),
            pltpu.VMEM((SLOTS, DEVS, WIDTH), BF16),
            pltpu.VMEM((2, SLOTS, CHIPS, WIDTH), BF16),
            pltpu.VMEM((2, 8, 128), F32),
            pltpu.VMEM((2, 8, 128), F32),
            pltpu.VMEM((2, SLOTS, GROUP, 128), BF16),
            pltpu.VMEM((3, 2, SLOTS, DEVS, GROUP), BF16),
            pltpu.VMEM((NX, 2, CHIPS // NX, 128), F32),
            pltpu.VMEM((2, CHIPS, 128), F32),
            pltpu.VMEM((2, CHIPS // NX, 128), F32),
            pltpu.VMEM((2, CHIPS, 128), F32),
            pltpu.VMEM((2, CHIPS, 128), F32),
            pltpu.VMEM((2, CHIPS, 128), F32),
            pltpu.VMEM((2, SLOTS, CHIPS, WIDTH), F32),
            pltpu.VMEM((2, SLOTS, CHIPS, WIDTH), BF16),
            pltpu.VMEM((2, SLOTS, CHIPS, WIDTH), BF16),
            pltpu.VMEM((2, DEVS, 128), F32),
            pltpu.VMEM((2, DEVS, 128), F32),
            pltpu.VMEM((2, 1, 128), F32),
            pltpu.VMEM((2, DEVS, 128), F32),
            pltpu.VMEM((Q, WIDTH), F32),
            pltpu.VMEM((ROWS, WIDTH), BF16),
            pltpu.VMEM((ROWS, 128), jnp.int32),
            pltpu.VMEM((ROWS, WIDTH), BF16),
            dma, dma, dma,
            dma((NZ,)), dma((NY,)),
            dma((CHIPS,)), dma, dma, dma, dma,
            dma, dma, dma, dma, dma,
            dma, dma((14,)), dma((7,)),
        ],
        compiler_params=pltpu.CompilerParams(collective_id=0, has_side_effects=True, vmem_limit_bytes=56 << 20),
        name="contrastive",
    )(ids.T, hidden, down, up, passages, storage.reshape(ROWS, 128))
    loss, ga, gb, table = pl.pallas_call(
        finish,
        out_shape=(shape((1, 1), F32), shape((RANK, WIDTH), F32), shape((RANK, WIDTH), F32), shape((ROWS, WIDTH), BF16)),
        in_specs=[vm, vm, hbm],
        out_specs=(vm, vm, vm, hbm),
        scratch_shapes=[pltpu.VMEM((ROWS, WIDTH), BF16), dma((4,)), dma((4,))],
        name="finish",
    )(loss, pieces, table)
    return loss.reshape(()), ga, gb, table


def solution(mesh):
    return jax.shard_map(
        shards,
        mesh=mesh,
        in_specs=(P("dp", "mp"), P(None, "mp"), P(None, "mp"), P("dp", "mp"), P("dp", None), P()),
        out_specs=(P(), P(None, "mp"), P(None, "mp"), P("dp", "mp")),
        check_vma=False,
    )
```

```python
import functools
import math

import jax
import jax.numpy as jnp
from jax import lax
from jax.experimental import pallas as pl
from jax.experimental.pallas import tpu as pltpu
from jax.sharding import PartitionSpec as P

SOFTMAX_TEMPER = 0.02
EPSILON = 1e-06
MESH = pl.DeviceIdType.MESH
F32, BF16 = jnp.float32, jnp.bfloat16
SLOTS = 3
NY = NZ = 8
NX = 4
Q = 24
LISTED = 8
RANK = 16
ROWS = 384
WIDTH = 1024
HALF = WIDTH // 2
TALL, SHORT = 16, 8
DEVS = 2 * NY * NZ
CHIPS = NY * NZ
GROUP = 16 * TALL
VOFF = SLOTS * Q
G_LANE, LOSS_LANE = 120, 121
TINY = 2.0**-80
NEG = -1e38


def nn(a, b):
    return lax.dot_general(a, b, (((1,), (0,)), ((), ())), preferred_element_type=F32)


def nt(a, b):
    return lax.dot_general(a, b, (((1,), (1,)), ((), ())), preferred_element_type=F32)


def tn(a, b):
    return lax.dot_general(a, b, (((0,), (0,)), ((), ())), preferred_element_type=F32)


def exact(dims, a, b):
    return lax.dot_general(a, b, (dims, ((), ())), preferred_element_type=F32, precision=lax.Precision.HIGHEST)


def split(x, parts):
    out = []
    for _ in range(parts):
        top = x.astype(BF16)
        out.append(top)
        x = x - top.astype(F32)
    return out


def iota(shape, dim):
    return lax.broadcasted_iota(jnp.int32, shape, dim)


def kernel(
    ids_hbm, hidden_hbm, down_hbm, up_hbm, pass_hbm, storage_hbm,
    loss_ref, pieces_ref, table_hbm,
    ids_ref, hidden_ref, down_ref, up_ref, hbuf, xb1, xb2, locs, lists, pick, picked, slots, flags, losses, folds, diag, rsx, part, summed, got, back, wrec,
    cand, cand_out, cand_all, piece_out, piece_in, piece_sum, final, mixed_ref, pass_ref, storage_ref, table_ref,
    e1_sem, e2_sem, l_sem, lz_sem, ly_sem, ring_sem, guest_sem, flag_sem, cand_sem, loss_sem, rsx_sem, got_sem, w_sem, rs_sem, ag_sem,
    send_sem, small_sem, load_sem,
):
    me, mp = lax.axis_index("dp"), lax.axis_index("mp")
    core, chip_me = lax.rem(me, 2), me // 2
    y, z = chip_me // NZ, lax.rem(chip_me, NZ)

    def dev(yy, zz, c):
        return ((lax.rem(yy + NY, NY) * NZ + lax.rem(zz + NZ, NZ)) * 2 + c, mp)

    def push(src, dst, ssem, rsem, target):
        pltpu.make_async_remote_copy(
            src_ref=src, dst_ref=dst, send_sem=ssem, recv_sem=rsem, device_id=target, device_id_type=MESH
        ).start()

    def take(ref, sem):
        pltpu.make_async_copy(ref, ref, sem).wait()

    sibling = (chip_me * 2 + 1 - core, mp)

    sa, sb = NZ - (NZ - 1) * core, 1 + (NZ - 1) * core
    a = jnp.where(core == 0, y, z)
    b = jnp.where(core == 0, z, y)

    def line_dev(o):
        return (lax.rem(a + o + NY, NY) * sa + b * sb) * 2 + core

    def cross_dev(o):
        return (a * sa + lax.rem(b + o + NY, NY) * sb) * 2 + core

    loads = [
        pltpu.make_async_copy(src, dst, load_sem.at[i])
        for i, (src, dst) in enumerate((
            (hidden_hbm, hidden_ref), (up_hbm, up_ref), (down_hbm, down_ref),
            (pass_hbm, pass_ref), (storage_hbm, storage_ref), (ids_hbm, ids_ref),
        ))
    ]
    loads[0].start()

    bar = pltpu.get_barrier_semaphore()
    for o in (4, 3, 5, 2, 6, 1, 7):
        pl.semaphore_signal(bar, inc=1, device_id=(line_dev(o), mp), device_id_type=MESH)
        pl.semaphore_signal(bar, inc=1, device_id=(cross_dev(o), mp), device_id_type=MESH)
    pl.semaphore_signal(bar, inc=1, device_id=sibling, device_id_type=MESH)
    for i in range(1, NX):
        pl.semaphore_signal(bar, inc=1, device_id=(me, lax.rem(mp + i, NX)), device_id_type=MESH)

    for cp in loads[1:]:
        cp.start()
    loads[0].wait()
    hid32 = hidden_ref[...].astype(F32)
    hbuf[chip_me, :, 0:WIDTH] = hid32[0:TALL].astype(BF16)
    folded = jnp.concatenate([hid32[TALL:Q, 0:HALF], hid32[TALL:Q, HALF:WIDTH]], axis=0)
    hbuf[chip_me, :, WIDTH : WIDTH + HALF] = folded.astype(BF16)
    pl.semaphore_wait(bar, NY - 1 + NZ - 1 + 1 + NX - 1)

    def chip_of(aa, bb):
        return lax.rem(aa + 2 * NY, NY) * sa + lax.rem(bb + 2 * NY, NY) * sb

    def pass_on(ci, target):
        push(hbuf.at[ci], hbuf.at[ci], send_sem, ring_sem.at[ci], (target, mp))

    for o in (-1, 1, -2, 2, -3, 3, 4):
        pass_on(chip_me, line_dev(o))
    ahead, behind = cross_dev(1), cross_dev(-1)
    offsets = (0, 1, -1, 2, -2, 3, -3, 4)

    def event(t, k):
        if t == 0:
            ci = chip_of(a + offsets[k], b)
            if k > 0:
                take(hbuf.at[ci], ring_sem.at[ci])
            pass_on(ci, ahead)
            pass_on(ci, behind)
            return
        for d in (1, -1):
            last = 4 if (k % 2 == 0) == (d > 0) else 3
            if t <= last:
                ci = chip_of(a + offsets[k], b - d * t)
                take(hbuf.at[ci], ring_sem.at[ci])
                if t < last:
                    pass_on(ci, ahead if d > 0 else behind)

    events = sorted(((t, k) for t in range(5) for k in range(NY)), key=lambda e: (e[0] == 4, 8 * e[0] + e[1]))

    def ring(first, last):
        for t, k in events[first:last]:
            event(t, k)

    loads[1].wait()
    loads[2].wait()
    up32 = up_ref[...].astype(F32)
    left = jnp.concatenate([hid32, up32], axis=0).astype(BF16)
    right = jnp.concatenate([down_ref[...].astype(F32), up32, jnp.zeros((96, WIDTH), F32)], axis=0).astype(BF16)
    prod = nt(left, right)

    loads[3].wait()
    biggest = jnp.max(jnp.max(jnp.abs(pass_ref[...].astype(F32)), axis=0, keepdims=True), axis=1, keepdims=True)
    lane40, row40 = iota((40, 128), 1), iota((40, 128), 0)
    xb1[mp] = jnp.where((lane40 == 40) & (row40 == 0), biggest, prod)
    for i in range(1, NX):
        push(xb1.at[mp], xb1.at[mp], small_sem.at[1], e1_sem, (me, lax.rem(mp + i, NX)))

    loads[4].wait()
    loads[5].wait()
    lane1 = iota((1, 128), 1)
    for j in range(Q * LISTED):
        pid = ids_ref[j % LISTED, j // LISTED]
        row = storage_ref[pl.ds(pid // 128, 1), :]
        locs[pl.ds(j, 1), :] = jnp.where(lane1 == lax.rem(pid, 128), row, 0).astype(F32)
    located = jnp.sum(locs[...], axis=1, keepdims=True)
    located = jnp.concatenate([located, jnp.full((64, 1), 1e6, F32)], axis=0)
    r256, l256 = iota((256, 256), 0), iota((256, 256), 1)
    as_row = jnp.sum(jnp.where(r256 == l256, located, 0.0), axis=0, keepdims=True)
    lists[0, core, pl.ds(chip_me, 1), :] = as_row[:, 0:128]
    lists[1, core, pl.ds(chip_me, 1), :] = as_row[:, 128:256]
    own_list = lists.at[:, core, pl.ds(chip_me, 1), :]
    push(own_list, own_list, small_sem.at[2], l_sem, sibling)

    take(lists.at[:, 0, pl.ds(0, 1), :], l_sem)

    def some_lists(first, n):
        return lists.at[:, :, pl.ds(pl.multiple_of(first, n), n), :]

    for o in (4, 3, 5, 2, 6, 1, 7):
        r = some_lists(chip_me, 1)
        push(r, r, small_sem.at[4], lz_sem.at[z], dev(y, z + o, core))

    def lists_on():
        def each(i, c):
            zz = lax.rem(z + i, NZ)
            take(some_lists(y * NZ + zz, 1), lz_sem.at[zz])
            return c
        lax.fori_loop(1, NZ, each, 0)
        for o in (4, 3, 5, 2, 6, 1, 7):
            r = some_lists(y * NZ, NZ)
            push(r, r, small_sem.at[5], ly_sem.at[y], dev(y + o, z, core))

    def lists_done():
        def each(i, c):
            yy = lax.rem(y + i, NY)
            take(some_lists(yy * NZ, NZ), ly_sem.at[yy])
            return c
        lax.fori_loop(1, NY, each, 0)

    ring(0, 8)

    take(xb1.at[pl.ds(0, NX - 1)], e1_sem)
    tot = xb1[0] + xb1[1] + xb1[2] + xb1[3]
    most = jnp.maximum(jnp.maximum(xb1[0], xb1[1]), jnp.maximum(xb1[2], xb1[3]))
    most = jnp.max(jnp.where((lane40 == 40) & (row40 == 0), most, 0.0))
    shrink = jnp.where(most > 2.0**40, TINY, 1.0)
    low_half = tot[0:Q, 0:RANK].astype(BF16)
    rolled = pltpu.roll(tot, 128 - RANK, 1)
    hid_up, gram = rolled[0:Q, 0:RANK], rolled[Q : Q + RANK, 0:RANK]
    mixed = hid32 + nn(low_half, up_ref[...])
    mixed_ref[...] = mixed
    xb2[mp] = jnp.broadcast_to(jnp.sum(mixed * mixed, axis=1, keepdims=True), (Q, 128))
    for i in range(1, NX):
        push(xb2.at[mp], xb2.at[mp], small_sem.at[3], e2_sem, (me, lax.rem(mp + i, NX)))

    flags[core] = jnp.full((8, 128), shrink, F32)
    push(flags.at[core], flags.at[core], small_sem.at[11], flag_sem, sibling)

    ring(8, 14)
    lists_on()
    ring(14, 24)

    take(xb2.at[pl.ds(0, NX - 1)], e2_sem)
    inv_norm = lax.rsqrt((xb2[0] + xb2[1] + xb2[2] + xb2[3]) / (WIDTH * NX) + EPSILON)

    ring(24, 32)
    lists_done()

    wanted = jnp.concatenate([lists[0].reshape(DEVS, 128), lists[1].reshape(DEVS, 128)], axis=1) - (me * ROWS).astype(F32)
    here = (wanted >= 0.0) & (wanted < ROWS)
    earlier = nn(here.astype(F32).astype(BF16), (r256 < l256).astype(F32).astype(BF16))
    rows_iota = iota((DEVS, ROWS), 1).astype(F32)
    for s in range(SLOTS):
        col = jnp.sum(jnp.where(here & (earlier == s), wanted + 1.0, 0.0), axis=1, keepdims=True) - 1.0
        pk = (rows_iota == col).astype(F32).astype(BF16)
        pick[s] = pk
        picked[s] = (nn(pk, pass_ref[...]) * shrink).astype(BF16)
    guests = pl.ds(pl.multiple_of((1 - core) * CHIPS, CHIPS), CHIPS)
    push(picked.at[:, guests, :], slots.at[core], small_sem.at[0], guest_sem, sibling)
    for s in range(SLOTS):
        slots[core, s] = picked[s, pl.ds(pl.multiple_of(core * CHIPS, CHIPS), CHIPS), :]

    ring(32, 36)
    lane = iota((DEVS, 128), 1)

    take(slots.at[0], guest_sem)
    take(flags.at[0], flag_sem)

    def slot_rows(s):
        return slots[:, s].reshape(DEVS, WIDTH)

    def up_lanes(s):
        return jnp.concatenate(
            [jnp.zeros((VOFF + s * RANK, WIDTH), F32), up32, jnp.zeros((128 - VOFF - (s + 1) * RANK, WIDTH), F32)], axis=0
        ).astype(BF16)

    part_pu = jnp.zeros((DEVS, 128), F32)
    for s in range(SLOTS):
        part_pu = part_pu + nt(slot_rows(s), up_lanes(s))

    ring(36, 40)

    quarter = CHIPS // NX
    for h in (0, 1):
        shrink_row = jnp.where(lane[0:CHIPS] == G_LANE, flags[h, 0:1, :] * (1.0 / NX), 0.0)
        part[h] = part_pu[h * CHIPS : (h + 1) * CHIPS, :] + shrink_row
    SG = 2 * SLOTS * 16
    block_t = lax.rem(iota((TALL, SG), 1), 16)
    block_s = lax.rem(iota((SHORT, SG), 1), 16)

    def tall(g):
        return hbuf[pl.ds(pl.multiple_of(g * 16, 16), 16), :, 0:WIDTH].reshape(GROUP, WIDTH)

    def short(g):
        return hbuf[pl.ds(pl.multiple_of(g * 16, 16), 16), :, WIDTH : WIDTH + HALF].reshape(GROUP, HALF)

    for i in range(1, NX + 1):
        g = lax.rem(mp + i, NX)
        rows = pl.ds(pl.multiple_of(g * 16, 16), 16)
        s_g = jnp.concatenate([slots[h, s, rows, :] for h in (0, 1) for s in range(SLOTS)], axis=0)
        d = nt(tall(g), s_g)
        d_lo, d_hi = nt(short(g), s_g[:, 0:HALF]), nt(short(g), s_g[:, HALF:WIDTH])
        e, f = jnp.zeros((TALL, SG), F32), jnp.zeros((SHORT, SG), F32)
        for r in range(16):
            at = r * TALL
            e = e + jnp.where(block_t == r, d[at : at + TALL, :], 0.0)
            f = f + jnp.where(block_s == r, d_lo[at : at + SHORT, :] + d_hi[at + SHORT : at + TALL, :], 0.0)
        e = jnp.concatenate([e, f], axis=0)
        e = jnp.concatenate([e, jnp.zeros((Q, 128 - SG), F32)], axis=1)
        e = jnp.transpose(jnp.concatenate([e, jnp.zeros((128 - Q, 128), F32)], axis=0))
        for h in (0, 1):
            at = h * SLOTS * 16
            one = e[at : at + 16, :] + pltpu.roll(e[at + 16 : at + 32, :], Q, 1) + pltpu.roll(e[at + 32 : at + 48, :], 2 * Q, 1)
            part[h, rows, :] = part[h, rows, :] + one
        if i < NX:
            push(part.at[:, rows, :], rsx.at[mp], small_sem.at[6], rsx_sem, (me, g))
        else:
            rsx[mp] = part[:, rows, :]

    take(rsx.at[pl.ds(0, NX - 1)], rsx_sem)
    summed[...] = rsx[0] + rsx[1] + rsx[2] + rsx[3]

    def swing(m):
        return ((8 - m) // 2) * (2 * lax.rem(m, 2) - 1)

    def far_first(m):
        return ((8 - m) // 2) * (1 if m % 2 else -1)

    def to_all(send, both):
        inner = [lax.rem(z + far_first(n) + NZ, NZ) for n in range(NZ)]
        cores = (1 - core, core) if both else (core,)

        def far_rows(m, carry):
            base = lax.rem(y + swing(m) + NY, NY) * NZ
            for n in inner:
                for c in cores:
                    send(base + n, c)
            return carry

        lax.fori_loop(0, NY - 1, far_rows, 0)
        for i, n in enumerate(inner):
            for c in cores[: len(cores) if i < NZ - 1 else len(cores) - 1]:
                send(y * NZ + n, c)

    def row_of(ref, chip):
        return ref.at[:, pl.ds(chip, 1), :]

    home = (chip_me // quarter) == mp
    others = [lax.rem(mp + dk, NX) for dk in (2, 1, 3)]

    def give(m, c):
        first = lax.rem(z + swing(m) + NZ, NZ)
        for j in (first, first + NZ):
            chip = mp * quarter + j
            for k in others:
                push(row_of(summed, j), row_of(got, chip_me), small_sem.at[7], got_sem, (chip * 2 + core, k))

            @pl.when(chip != chip_me)
            def _():
                push(row_of(summed, j), row_of(got, chip_me), small_sem.at[7], got_sem, (chip * 2 + core, mp))
        return c

    lax.fori_loop(0, NZ, give, 0)

    @pl.when(home)
    def _():
        pltpu.make_async_copy(row_of(summed, lax.rem(chip_me, quarter)), row_of(got, chip_me), got_sem).start()

    owner = jnp.floor((located + 0.5) * (1.0 / ROWS))
    owner_chip = jnp.floor(owner * 0.5)
    owner = (owner - 2.0 * owner_chip) * CHIPS + owner_chip
    hold = (iota((256, 128), 1).astype(F32) == owner).astype(F32)
    hold_b = hold.astype(BF16)
    rank = jnp.sum(hold * nn((r256 > l256).astype(F32).astype(BF16), hold_b), axis=1, keepdims=True)
    count = tn(hold_b, jnp.ones((256, 128), BF16))
    l_col = iota((256, 128), 1)
    pos_at = (iota((256, 128), 0) == LISTED * lax.rem(l_col, Q)) & (rank == (l_col // Q).astype(F32)) & (l_col < VOFF)
    positive = tn(hold_b, pos_at.astype(F32).astype(BF16))
    valid = (count > (lane // Q).astype(F32)) & (lane < VOFF)

    row128 = iota((128, RANK), 0)
    at_rank = ((row128 >= VOFF) & (row128 < VOFF + SLOTS * RANK) & (lax.rem(row128 - VOFF + 128 * RANK, RANK) == iota((128, RANK), 1)))
    at_rank = at_rank.astype(F32)
    at_query = ((iota((Q, 128), 1) < VOFF) & (lax.rem(iota((Q, 128), 1), Q) == iota((Q, 128), 0))).astype(F32)
    spread = nn(nt(at_rank.astype(BF16), low_half).astype(BF16), at_query.astype(BF16))
    row_a, lane_a = iota((128, 128), 0), iota((128, 128), 1)
    same_slot = ((row_a + 128 * RANK - VOFF) // RANK - 128) == lane_a // Q
    spread = jnp.where(same_slot, spread, 0.0).astype(BF16)
    inv_lane = jnp.sum(inv_norm * at_query, axis=0, keepdims=True)

    for s in range(SLOTS):
        f_lane = iota((GROUP, 128), 1) - s * Q
        f_row = iota((GROUP, 128), 0)
        folds[0, s] = (f_lane == lax.rem(f_row, TALL)).astype(F32).astype(BF16)
        folds[1, s] = (f_lane == TALL + lax.rem(f_row, SHORT)).astype(F32).astype(BF16)
    take(got, got_sem)

    g = got[...].reshape(DEVS, 128)
    unshrink = jnp.sum(jnp.where(lane == G_LANE, g, 0.0), axis=1, keepdims=True)
    unshrink = jnp.where(unshrink < 0.5, 1.0 / TINY, 1.0)
    ranks = jnp.where((lane >= VOFF) & (lane < VOFF + SLOTS * RANK), g, 0.0)
    raw = g
    for piece in split(ranks, 3):
        raw = raw + nn(piece, spread)
    raw = jnp.where(valid & (inv_lane > 0.0), raw * inv_lane * unshrink, 0.0)
    scale = 1.0 / (SOFTMAX_TEMPER * math.sqrt(WIDTH * NX))
    scores = jnp.where(valid, raw * scale, NEG)

    def over_slots(x, op, fill):
        x0 = op(op(x, pltpu.roll(x, 128 - Q, 1)), pltpu.roll(x, 128 - 2 * Q, 1))
        return jnp.where(lane1 < Q, x0, jnp.where(lane1 < 2 * Q, pltpu.roll(x0, Q, 1), jnp.where(lane1 < 3 * Q, pltpu.roll(x0, 2 * Q, 1), fill)))

    top = over_slots(jnp.max(scores, axis=0, keepdims=True), jnp.maximum, 0.0)
    expo = jnp.where(valid, jnp.exp(scores - top), 0.0)
    total = over_slots(jnp.sum(expo, axis=0, keepdims=True), jnp.add, 1.0)
    own = over_slots(jnp.sum(jnp.where(positive > 0.5, scores, 0.0), axis=0, keepdims=True), jnp.add, 0.0)
    loss = jnp.sum(jnp.where(lane1 < Q, jnp.log(total) + top - own, 0.0), axis=1, keepdims=True)
    weights = jnp.where(valid, (expo / total - positive) * scale, 0.0)
    tangent = over_slots(jnp.sum(weights * raw, axis=0, keepdims=True), jnp.add, 0.0) / (WIDTH * NX)
    w2 = weights * inv_lane
    v = jnp.zeros((DEVS, 128), F32)
    for piece in split(w2, 3):
        v = v + nt(piece, spread)
    back[...] = (w2 + v + jnp.where(lane == LOSS_LANE, loss, 0.0)).reshape(2, CHIPS, 128)

    to_all(lambda chip, c: push(row_of(back, chip), row_of(wrec, chip_me), small_sem.at[8], w_sem, (chip * 2 + c, mp)), False)
    pltpu.make_async_copy(row_of(back, chip_me), row_of(wrec, chip_me), w_sem).start()

    z_all = exact(((0,), (0,)), weights, ranks * unshrink)
    z_all = jnp.where(lane_a >= VOFF, z_all, 0.0)
    same_t = ((lane_a + 128 * RANK - VOFF) // RANK - 128) == row_a // Q
    z_all = jnp.where(same_t, z_all, 0.0)
    w_pu = exact(((1,), (0,)), exact(((1,), (0,)), at_query, z_all), at_rank)
    inv_col = inv_norm[:, 0:1]
    q_up = inv_col * (hid_up + exact(((1,), (0,)), low_half.astype(F32), gram))
    tan_col = jnp.sum(jnp.where((iota((Q, 128), 1) < Q), at_query, 0.0) * tangent, axis=1, keepdims=True)
    low_grad = (inv_col * (w_pu - tan_col * q_up)).astype(BF16)
    ga = tn(low_grad, hidden_ref[...])
    pulled = (mixed_ref[...] * (inv_col * inv_col * tan_col)).astype(BF16)
    gb = -tn(low_half, pulled)

    for j in range(WIDTH // 128):
        piece_out[0, pl.ds(j * RANK, RANK), :] = ga[:, j * 128 : (j + 1) * 128]

    take(wrec, w_sem)
    w = wrec[...].reshape(DEVS, 128)
    lost = jnp.where((lane == LOSS_LANE) & (iota((DEVS, 128), 0) < CHIPS), w, 0.0)
    losses[core] = jnp.broadcast_to(jnp.sum(jnp.sum(lost, axis=0, keepdims=True), axis=1, keepdims=True), (8, 128))
    push(losses.at[core], losses.at[core], small_sem.at[13], loss_sem, sibling)
    w_t = jnp.transpose(w) * jnp.where(lane1 < CHIPS, 1.0 / flags[0, 0:1, :], 1.0 / flags[1, 0:1, :])
    for s in range(SLOTS):
        v_hi, v_lo = split(w_t[VOFF + s * RANK : VOFF + (s + 1) * RANK, :], 2)
        r = nn(jnp.concatenate([v_hi, v_lo], axis=0), slot_rows(s))
        gb = gb + r[0:RANK] + r[RANK : 2 * RANK]
    for j in range(WIDTH // 128):
        piece_out[1, pl.ds(j * RANK, RANK), :] = gb[:, j * 128 : (j + 1) * 128]

    to_all(lambda chip, c: push(row_of(piece_out, chip * 2 + c), row_of(piece_in, me), small_sem.at[9], rs_sem, (chip * 2 + c, mp)), True)
    pltpu.make_async_copy(piece_out.at[:, pl.ds(me, 1), :], piece_in.at[:, pl.ds(me, 1), :], rs_sem).start()

    hi, lo = split(w, 2)
    d_lane = iota((DEVS, GROUP), 1)
    wide = (d_lane // TALL) == lax.rem(iota((DEVS, GROUP), 0), 16)
    first_half = lax.rem(d_lane // SHORT, 2) == 0
    for s in range(SLOTS):
        for i, piece in enumerate((hi, lo)):
            diag[0, i, s] = jnp.where(wide, nt(piece, folds[0, s]), 0.0).astype(BF16)
            low8 = jnp.where(wide, nt(piece, folds[1, s]), 0.0)
            diag[1, i, s] = jnp.where(first_half, low8, 0.0).astype(BF16)
            diag[2, i, s] = jnp.where(first_half, 0.0, low8).astype(BF16)

    def candidates(g_, c):
        rows = pl.ds(pl.multiple_of(g_ * 16, 16), 16)
        d0, d1, d2 = (
            jnp.concatenate(
                [diag[n, i, s, pl.ds(pl.multiple_of(h * CHIPS + g_ * 16, 16), 16), :] for i in (0, 1) for h in (0, 1) for s in range(SLOTS)],
                axis=0,
            )
            for n in range(3)
        )
        o = nn(d0, tall(g_)) + jnp.concatenate([nn(d1, short(g_)), nn(d2, short(g_))], axis=1)
        o = o[0:SG, :] + o[SG : 2 * SG, :]
        for h in (0, 1):
            for s in range(SLOTS):
                at = (h * SLOTS + s) * 16
                cand[h, s, rows, :] = o[at : at + 16, :]
        return c

    lax.fori_loop(0, CHIPS // 16, candidates, 0)
    for s in range(SLOTS):
        up_at = up_lanes(s)
        cg = cand[:, s].reshape(DEVS, WIDTH) + nn(hi, up_at) + nn(lo, up_at)
        cand_out[:, s] = cg.astype(BF16).reshape(2, CHIPS, WIDTH)
    push(cand_out.at[1 - core], cand_all.at[core], small_sem.at[12], cand_sem, sibling)
    cand_all[core] = cand_out[core]

    take(piece_in, rs_sem)
    piece_sum[...] = jnp.sum(piece_in[...], axis=1, keepdims=True)
    final[:, pl.ds(me, 1), :] = piece_sum[...]

    to_all(lambda chip, c: push(piece_sum, row_of(final, me), small_sem.at[10], ag_sem, (chip * 2 + c, mp)), True)
    take(cand_all.at[0], cand_sem)
    table = jnp.zeros((ROWS, WIDTH), F32)
    for s in range(SLOTS):
        table = table + tn(pick[s], cand_all[:, s].reshape(DEVS, WIDTH))
    table_ref[...] = table.astype(BF16)
    table_out = pltpu.make_async_copy(table_ref, table_hbm, load_sem.at[6])
    table_out.start()

    take(final.at[:, pl.ds(0, DEVS - 1), :], ag_sem)
    pieces_ref[...] = final[...]
    take(losses.at[0], loss_sem)
    loss_ref[...] = (losses[0, 0:1, 0:1] + losses[1, 0:1, 0:1]) / (DEVS * Q)
    table_out.wait()

    take(hbuf.at[pl.ds(0, CHIPS - 1)], send_sem)
    take(picked.at[:, pl.ds(0, CHIPS), :], small_sem.at[0])
    take(xb1.at[pl.ds(0, NX - 1)], small_sem.at[1])
    take(lists.at[:, 0, pl.ds(0, 1), :], small_sem.at[2])
    take(xb2.at[pl.ds(0, NX - 1)], small_sem.at[3])
    take(lists.at[:, :, pl.ds(0, NZ - 1), :], small_sem.at[4])
    take(lists.at[:, :, pl.ds(0, NZ * (NY - 1)), :], small_sem.at[5])
    take(rsx.at[pl.ds(0, NX - 1)], small_sem.at[6])
    @pl.when(home)
    def _():
        take(got.at[:, pl.ds(0, CHIPS - 1), :], small_sem.at[7])

    @pl.when(jnp.logical_not(home))
    def _():
        take(got, small_sem.at[7])

    take(wrec.at[:, pl.ds(0, CHIPS - 1), :], small_sem.at[8])
    take(piece_in.at[:, pl.ds(0, DEVS - 1), :], small_sem.at[9])
    take(final.at[:, pl.ds(0, DEVS - 1), :], small_sem.at[10])
    take(flags.at[0], small_sem.at[11])
    take(losses.at[0], small_sem.at[13])
    take(cand_out.at[0], small_sem.at[12])


def finish(loss_in, pieces_ref, table_in, loss_ref, ga_ref, gb_ref, table_out):
    table_out[...] = table_in[...]

    @pl.when(pl.program_id(0) == 0)
    def _():
        loss_ref[...] = loss_in[...]
        for j in range(WIDTH // 128):
            ga_ref[:, pl.ds(j * 128, 128)] = pieces_ref[0, pl.ds(j * RANK, RANK), :]
            gb_ref[:, pl.ds(j * 128, 128)] = pieces_ref[1, pl.ds(j * RANK, RANK), :]


def shards(hidden, down, up, passages, ids, storage):
    vm, hbm = pl.BlockSpec(memory_space=pltpu.VMEM), pl.BlockSpec(memory_space=pl.ANY)
    dma = pltpu.SemaphoreType.DMA
    shape = jax.ShapeDtypeStruct
    loss, pieces, table = pl.pallas_call(
        kernel,
        out_shape=(shape((1, 1), F32), shape((2, DEVS, 128), F32), shape((ROWS, WIDTH), BF16)),
        in_specs=[hbm] * 6,
        out_specs=(vm, vm, hbm),
        scratch_shapes=[
            pltpu.SMEM((LISTED, Q), jnp.int32),
            pltpu.VMEM((Q, WIDTH), BF16),
            pltpu.VMEM((RANK, WIDTH), BF16),
            pltpu.VMEM((RANK, WIDTH), BF16),
            pltpu.VMEM((CHIPS, TALL, WIDTH + HALF), BF16),
            pltpu.VMEM((NX, 40, 128), F32),
            pltpu.VMEM((NX, Q, 128), F32),
            pltpu.VMEM((Q * LISTED, 128), F32),
            pltpu.VMEM((2, 2, CHIPS, 128), F32),
            pltpu.VMEM((SLOTS, DEVS, ROWS), BF16),
            pltpu.VMEM((SLOTS, DEVS, WIDTH), BF16),
            pltpu.VMEM((2, SLOTS, CHIPS, WIDTH), BF16),
            pltpu.VMEM((2, 8, 128), F32),
            pltpu.VMEM((2, 8, 128), F32),
            pltpu.VMEM((2, SLOTS, GROUP, 128), BF16),
            pltpu.VMEM((3, 2, SLOTS, DEVS, GROUP), BF16),
            pltpu.VMEM((NX, 2, CHIPS // NX, 128), F32),
            pltpu.VMEM((2, CHIPS, 128), F32),
            pltpu.VMEM((2, CHIPS // NX, 128), F32),
            pltpu.VMEM((2, CHIPS, 128), F32),
            pltpu.VMEM((2, CHIPS, 128), F32),
            pltpu.VMEM((2, CHIPS, 128), F32),
            pltpu.VMEM((2, SLOTS, CHIPS, WIDTH), F32),
            pltpu.VMEM((2, SLOTS, CHIPS, WIDTH), BF16),
            pltpu.VMEM((2, SLOTS, CHIPS, WIDTH), BF16),
            pltpu.VMEM((2, DEVS, 128), F32),
            pltpu.VMEM((2, DEVS, 128), F32),
            pltpu.VMEM((2, 1, 128), F32),
            pltpu.VMEM((2, DEVS, 128), F32),
            pltpu.VMEM((Q, WIDTH), F32),
            pltpu.VMEM((ROWS, WIDTH), BF16),
            pltpu.VMEM((ROWS, 128), jnp.int32),
            pltpu.VMEM((ROWS, WIDTH), BF16),
            dma, dma, dma,
            dma((NZ,)), dma((NY,)),
            dma((CHIPS,)), dma, dma, dma, dma,
            dma, dma, dma, dma, dma,
            dma, dma((14,)), dma((7,)),
        ],
        compiler_params=pltpu.CompilerParams(collective_id=0, has_side_effects=True, vmem_limit_bytes=56 << 20),
        name="contrastive",
    )(ids.T, hidden, down, up, passages, storage.reshape(ROWS, 128))
    rows = pl.BlockSpec((ROWS // 2, WIDTH), lambda i: (i, 0))

    def whole(*dims):
        return pl.BlockSpec(dims, lambda i: (0,) * len(dims))

    loss, ga, gb, table = pl.pallas_call(
        finish,
        out_shape=(shape((1, 1), F32), shape((RANK, WIDTH), F32), shape((RANK, WIDTH), F32), shape((ROWS, WIDTH), BF16)),
        grid=(2,),
        in_specs=[whole(1, 1), whole(2, DEVS, 128), rows],
        out_specs=(whole(1, 1), whole(RANK, WIDTH), whole(RANK, WIDTH), rows),
        name="finish",
    )(loss, pieces, table)
    return loss.reshape(()), ga, gb, table


def solution(mesh):
    return jax.shard_map(
        shards,
        mesh=mesh,
        in_specs=(P("dp", "mp"), P(None, "mp"), P(None, "mp"), P("dp", "mp"), P("dp", None), P()),
        out_specs=(P(), P(None, "mp"), P(None, "mp"), P("dp", "mp")),
        check_vma=False,
    )
```

```python
import functools
import math

import jax
import jax.numpy as jnp
from jax import lax
from jax.experimental import pallas as pl
from jax.experimental.pallas import tpu as pltpu
from jax.sharding import PartitionSpec as P

SOFTMAX_TEMPER = 0.02
EPSILON = 1e-06
MESH = pl.DeviceIdType.MESH
F32, BF16 = jnp.float32, jnp.bfloat16
SLOTS = 3
NY = NZ = 8
NX = 4
Q = 24
LISTED = 8
RANK = 16
ROWS = 384
WIDTH = 1024
HALF = WIDTH // 2
TALL, SHORT = 16, 8
DEVS = 2 * NY * NZ
CHIPS = NY * NZ
GROUP = 16 * TALL
VOFF = SLOTS * Q
G_LANE, LOSS_LANE = 120, 121
TINY = 2.0**-80
NEG = -1e38


def nn(a, b):
    return lax.dot_general(a, b, (((1,), (0,)), ((), ())), preferred_element_type=F32)


def nt(a, b):
    return lax.dot_general(a, b, (((1,), (1,)), ((), ())), preferred_element_type=F32)


def tn(a, b):
    return lax.dot_general(a, b, (((0,), (0,)), ((), ())), preferred_element_type=F32)


def exact(dims, a, b):
    return lax.dot_general(a, b, (dims, ((), ())), preferred_element_type=F32, precision=lax.Precision.HIGHEST)


def split(x, parts):
    out = []
    for _ in range(parts):
        top = x.astype(BF16)
        out.append(top)
        x = x - top.astype(F32)
    return out


def iota(shape, dim):
    return lax.broadcasted_iota(jnp.int32, shape, dim)


def kernel(
    ids_hbm, hidden_hbm, down_hbm, up_hbm, pass_hbm, storage_hbm,
    loss_ref, pieces_ref, table_hbm,
    ids_ref, hidden_ref, down_ref, up_ref, hbuf, xb1, xb2, locs, lists, pick, picked, slots, flags, losses, folds, diag, rsx, part, summed, got, back, wrec,
    cand, cand_out, cand_all, piece_out, piece_in, piece_sum, final, mixed_ref, pass_ref, storage_ref, table_ref,
    e1_sem, e2_sem, l_sem, lz_sem, ly_sem, ring_sem, guest_sem, flag_sem, cand_sem, loss_sem, rsx_sem, got_sem, w_sem, rs_sem, ag_sem,
    send_sem, small_sem, load_sem,
):
    me, mp = lax.axis_index("dp"), lax.axis_index("mp")
    core, chip_me = lax.rem(me, 2), me // 2
    y, z = chip_me // NZ, lax.rem(chip_me, NZ)

    def dev(yy, zz, c):
        return ((lax.rem(yy + NY, NY) * NZ + lax.rem(zz + NZ, NZ)) * 2 + c, mp)

    def push(src, dst, ssem, rsem, target):
        pltpu.make_async_remote_copy(
            src_ref=src, dst_ref=dst, send_sem=ssem, recv_sem=rsem, device_id=target, device_id_type=MESH
        ).start()

    def take(ref, sem):
        pltpu.make_async_copy(ref, ref, sem).wait()

    sibling = (chip_me * 2 + 1 - core, mp)

    sa, sb = NZ - (NZ - 1) * core, 1 + (NZ - 1) * core
    a = jnp.where(core == 0, y, z)
    b = jnp.where(core == 0, z, y)

    def line_dev(o):
        return (lax.rem(a + o + NY, NY) * sa + b * sb) * 2 + core

    def cross_dev(o):
        return (a * sa + lax.rem(b + o + NY, NY) * sb) * 2 + core

    loads = [
        pltpu.make_async_copy(src, dst, load_sem.at[i])
        for i, (src, dst) in enumerate((
            (hidden_hbm, hidden_ref), (up_hbm, up_ref), (down_hbm, down_ref),
            (pass_hbm, pass_ref), (storage_hbm, storage_ref), (ids_hbm, ids_ref),
        ))
    ]
    loads[0].start()

    bar = pltpu.get_barrier_semaphore()
    for o in (4, 3, 5, 2, 6, 1, 7):
        pl.semaphore_signal(bar, inc=1, device_id=(line_dev(o), mp), device_id_type=MESH)
        pl.semaphore_signal(bar, inc=1, device_id=(cross_dev(o), mp), device_id_type=MESH)
    pl.semaphore_signal(bar, inc=1, device_id=sibling, device_id_type=MESH)
    for i in range(1, NX):
        pl.semaphore_signal(bar, inc=1, device_id=(me, lax.rem(mp + i, NX)), device_id_type=MESH)

    for cp in loads[1:]:
        cp.start()
    loads[0].wait()
    hid32 = hidden_ref[...].astype(F32)
    hbuf[chip_me, :, 0:WIDTH] = hid32[0:TALL].astype(BF16)
    folded = jnp.concatenate([hid32[TALL:Q, 0:HALF], hid32[TALL:Q, HALF:WIDTH]], axis=0)
    hbuf[chip_me, :, WIDTH : WIDTH + HALF] = folded.astype(BF16)
    pl.semaphore_wait(bar, NY - 1 + NZ - 1 + 1 + NX - 1)

    def chip_of(aa, bb):
        return lax.rem(aa + 2 * NY, NY) * sa + lax.rem(bb + 2 * NY, NY) * sb

    def pass_on(ci, target):
        push(hbuf.at[ci], hbuf.at[ci], send_sem, ring_sem.at[ci], (target, mp))

    for o in (-1, 1, -2, 2, -3, 3, 4):
        pass_on(chip_me, line_dev(o))
    ahead, behind = cross_dev(1), cross_dev(-1)
    offsets = (0, 1, -1, 2, -2, 3, -3, 4)

    def event(t, k):
        if t == 0:
            ci = chip_of(a + offsets[k], b)
            if k > 0:
                take(hbuf.at[ci], ring_sem.at[ci])
            pass_on(ci, ahead)
            pass_on(ci, behind)
            return
        for d in (1, -1):
            last = 4 if (k % 2 == 0) == (d > 0) else 3
            if t <= last:
                ci = chip_of(a + offsets[k], b - d * t)
                take(hbuf.at[ci], ring_sem.at[ci])
                if t < last:
                    pass_on(ci, ahead if d > 0 else behind)

    events = sorted(((t, k) for t in range(5) for k in range(NY)), key=lambda e: (e[0] == 4, 8 * e[0] + e[1]))

    def ring(first, last):
        for t, k in events[first:last]:
            event(t, k)

    loads[1].wait()
    loads[2].wait()
    up32 = up_ref[...].astype(F32)
    left = jnp.concatenate([hid32, up32], axis=0).astype(BF16)
    right = jnp.concatenate([down_ref[...].astype(F32), up32, jnp.zeros((96, WIDTH), F32)], axis=0).astype(BF16)
    prod = nt(left, right)

    loads[3].wait()
    biggest = jnp.max(jnp.max(jnp.abs(pass_ref[...].astype(F32)), axis=0, keepdims=True), axis=1, keepdims=True)
    lane40, row40 = iota((40, 128), 1), iota((40, 128), 0)
    xb1[mp] = jnp.where((lane40 == 40) & (row40 == 0), biggest, prod)
    for i in range(1, NX):
        push(xb1.at[mp], xb1.at[mp], small_sem.at[1], e1_sem, (me, lax.rem(mp + i, NX)))

    loads[4].wait()
    loads[5].wait()
    lane1 = iota((1, 128), 1)
    for j in range(Q * LISTED):
        pid = ids_ref[j % LISTED, j // LISTED]
        row = storage_ref[pl.ds(pid // 128, 1), :]
        locs[pl.ds(j, 1), :] = jnp.where(lane1 == lax.rem(pid, 128), row, 0).astype(F32)
    located = jnp.sum(locs[...], axis=1, keepdims=True)
    located = jnp.concatenate([located, jnp.full((64, 1), 1e6, F32)], axis=0)
    r256, l256 = iota((256, 256), 0), iota((256, 256), 1)
    as_row = jnp.sum(jnp.where(r256 == l256, located, 0.0), axis=0, keepdims=True)
    lists[0, core, pl.ds(chip_me, 1), :] = as_row[:, 0:128]
    lists[1, core, pl.ds(chip_me, 1), :] = as_row[:, 128:256]
    own_list = lists.at[:, core, pl.ds(chip_me, 1), :]
    push(own_list, own_list, small_sem.at[2], l_sem, sibling)

    take(lists.at[:, 0, pl.ds(0, 1), :], l_sem)

    def some_lists(first, n):
        return lists.at[:, :, pl.ds(pl.multiple_of(first, n), n), :]

    for o in (4, 3, 5, 2, 6, 1, 7):
        r = some_lists(chip_me, 1)
        push(r, r, small_sem.at[4], lz_sem.at[z], dev(y, z + o, core))

    def lists_on():
        def each(i, c):
            zz = lax.rem(z + i, NZ)
            take(some_lists(y * NZ + zz, 1), lz_sem.at[zz])
            return c
        lax.fori_loop(1, NZ, each, 0)
        for o in (4, 3, 5, 2, 6, 1, 7):
            r = some_lists(y * NZ, NZ)
            push(r, r, small_sem.at[5], ly_sem.at[y], dev(y + o, z, core))

    def lists_done():
        def each(i, c):
            yy = lax.rem(y + i, NY)
            take(some_lists(yy * NZ, NZ), ly_sem.at[yy])
            return c
        lax.fori_loop(1, NY, each, 0)

    ring(0, 8)

    take(xb1.at[pl.ds(0, NX - 1)], e1_sem)
    tot = xb1[0] + xb1[1] + xb1[2] + xb1[3]
    most = jnp.maximum(jnp.maximum(xb1[0], xb1[1]), jnp.maximum(xb1[2], xb1[3]))
    most = jnp.max(jnp.where((lane40 == 40) & (row40 == 0), most, 0.0))
    shrink = jnp.where(most > 2.0**40, TINY, 1.0)
    low_half = tot[0:Q, 0:RANK].astype(BF16)
    rolled = pltpu.roll(tot, 128 - RANK, 1)
    hid_up, gram = rolled[0:Q, 0:RANK], rolled[Q : Q + RANK, 0:RANK]
    mixed = hid32 + nn(low_half, up_ref[...])
    mixed_ref[...] = mixed
    xb2[mp] = jnp.broadcast_to(jnp.sum(mixed * mixed, axis=1, keepdims=True), (Q, 128))
    for i in range(1, NX):
        push(xb2.at[mp], xb2.at[mp], small_sem.at[3], e2_sem, (me, lax.rem(mp + i, NX)))

    flags[core] = jnp.full((8, 128), shrink, F32)
    push(flags.at[core], flags.at[core], small_sem.at[11], flag_sem, sibling)

    ring(8, 14)
    lists_on()
    ring(14, 24)

    take(xb2.at[pl.ds(0, NX - 1)], e2_sem)
    inv_norm = lax.rsqrt((xb2[0] + xb2[1] + xb2[2] + xb2[3]) / (WIDTH * NX) + EPSILON)

    ring(24, 32)
    lists_done()

    wanted = jnp.concatenate([lists[0].reshape(DEVS, 128), lists[1].reshape(DEVS, 128)], axis=1) - (me * ROWS).astype(F32)
    here = (wanted >= 0.0) & (wanted < ROWS)
    earlier = nn(here.astype(F32).astype(BF16), (r256 < l256).astype(F32).astype(BF16))
    rows_iota = iota((DEVS, ROWS), 1).astype(F32)
    for s in range(SLOTS):
        col = jnp.sum(jnp.where(here & (earlier == s), wanted + 1.0, 0.0), axis=1, keepdims=True) - 1.0
        pk = (rows_iota == col).astype(F32).astype(BF16)
        pick[s] = pk
        picked[s] = (nn(pk, pass_ref[...]) * shrink).astype(BF16)
    guests = pl.ds(pl.multiple_of((1 - core) * CHIPS, CHIPS), CHIPS)
    push(picked.at[:, guests, :], slots.at[core], small_sem.at[0], guest_sem, sibling)
    for s in range(SLOTS):
        slots[core, s] = picked[s, pl.ds(pl.multiple_of(core * CHIPS, CHIPS), CHIPS), :]

    ring(32, 36)
    lane = iota((DEVS, 128), 1)

    take(slots.at[0], guest_sem)
    take(flags.at[0], flag_sem)

    def slot_rows(s):
        return slots[:, s].reshape(DEVS, WIDTH)

    def up_lanes(s):
        return jnp.concatenate(
            [jnp.zeros((VOFF + s * RANK, WIDTH), F32), up32, jnp.zeros((128 - VOFF - (s + 1) * RANK, WIDTH), F32)], axis=0
        ).astype(BF16)

    part_pu = jnp.zeros((DEVS, 128), F32)
    for s in range(SLOTS):
        part_pu = part_pu + nt(slot_rows(s), up_lanes(s))

    ring(36, 40)

    quarter = CHIPS // NX
    for h in (0, 1):
        shrink_row = jnp.where(lane[0:CHIPS] == G_LANE, flags[h, 0:1, :] * (1.0 / NX), 0.0)
        part[h] = part_pu[h * CHIPS : (h + 1) * CHIPS, :] + shrink_row
    SG = 2 * SLOTS * 16
    block_t = lax.rem(iota((TALL, SG), 1), 16)
    block_s = lax.rem(iota((SHORT, SG), 1), 16)

    def tall(g):
        return hbuf[pl.ds(pl.multiple_of(g * 16, 16), 16), :, 0:WIDTH].reshape(GROUP, WIDTH)

    def short(g):
        return hbuf[pl.ds(pl.multiple_of(g * 16, 16), 16), :, WIDTH : WIDTH + HALF].reshape(GROUP, HALF)

    for i in range(1, NX + 1):
        g = lax.rem(mp + i, NX)
        rows = pl.ds(pl.multiple_of(g * 16, 16), 16)
        s_g = jnp.concatenate([slots[h, s, rows, :] for h in (0, 1) for s in range(SLOTS)], axis=0)
        d = nt(tall(g), s_g)
        d_lo, d_hi = nt(short(g), s_g[:, 0:HALF]), nt(short(g), s_g[:, HALF:WIDTH])
        e, f = jnp.zeros((TALL, SG), F32), jnp.zeros((SHORT, SG), F32)
        for r in range(16):
            at = r * TALL
            e = e + jnp.where(block_t == r, d[at : at + TALL, :], 0.0)
            f = f + jnp.where(block_s == r, d_lo[at : at + SHORT, :] + d_hi[at + SHORT : at + TALL, :], 0.0)
        e = jnp.concatenate([e, f], axis=0)
        e = jnp.concatenate([e, jnp.zeros((Q, 128 - SG), F32)], axis=1)
        e = jnp.transpose(jnp.concatenate([e, jnp.zeros((128 - Q, 128), F32)], axis=0))
        for h in (0, 1):
            at = h * SLOTS * 16
            one = e[at : at + 16, :] + pltpu.roll(e[at + 16 : at + 32, :], Q, 1) + pltpu.roll(e[at + 32 : at + 48, :], 2 * Q, 1)
            part[h, rows, :] = part[h, rows, :] + one
        if i < NX:
            push(part.at[:, rows, :], rsx.at[mp], small_sem.at[6], rsx_sem, (me, g))
        else:
            rsx[mp] = part[:, rows, :]

    take(rsx.at[pl.ds(0, NX - 1)], rsx_sem)
    summed[...] = rsx[0] + rsx[1] + rsx[2] + rsx[3]

    def swing(m):
        return ((8 - m) // 2) * (2 * lax.rem(m, 2) - 1)

    def far_first(m):
        return ((8 - m) // 2) * (1 if m % 2 else -1)

    def hops(o):
        return min(o % NY, NY - o % NY)

    paths = sorted(((dy, dz) for dy in range(NY) for dz in range(NZ)), key=lambda w: -hops(w[0]) - hops(w[1]))

    def to_all(send, both):
        rows_y = [lax.rem(y + o, NY) * NZ for o in range(NY)]
        cols_z = [lax.rem(z + o, NZ) for o in range(NZ)]
        for dy, dz in paths:
            for c in (1 - core, core) if both else (core,):
                if dy + dz > 0 or (both and c is not core):
                    send(rows_y[dy] + cols_z[dz], c)

    def row_of(ref, chip):
        return ref.at[:, pl.ds(chip, 1), :]

    home = (chip_me // quarter) == mp
    ways = sorted(((dz, dk) for dz in range(NZ) for dk in range(NX)), key=lambda w: -hops(w[0]) - min(w[1], NX - w[1]))
    for dz, dk in ways:
        for dy in (0, 1):
            j = dy * NZ + lax.rem(z + dz, NZ)
            chip = mp * quarter + j
            if dz + dk > 0:
                push(row_of(summed, j), row_of(got, chip_me), small_sem.at[7], got_sem, (chip * 2 + core, lax.rem(mp + dk, NX)))
            else:
                @pl.when(chip != chip_me)
                def _():
                    push(row_of(summed, j), row_of(got, chip_me), small_sem.at[7], got_sem, (chip * 2 + core, mp))

    @pl.when(home)
    def _():
        pltpu.make_async_copy(row_of(summed, lax.rem(chip_me, quarter)), row_of(got, chip_me), got_sem).start()

    owner = jnp.floor((located + 0.5) * (1.0 / ROWS))
    owner_chip = jnp.floor(owner * 0.5)
    owner = (owner - 2.0 * owner_chip) * CHIPS + owner_chip
    hold = (iota((256, 128), 1).astype(F32) == owner).astype(F32)
    hold_b = hold.astype(BF16)
    rank = jnp.sum(hold * nn((r256 > l256).astype(F32).astype(BF16), hold_b), axis=1, keepdims=True)
    count = tn(hold_b, jnp.ones((256, 128), BF16))
    l_col = iota((256, 128), 1)
    pos_at = (iota((256, 128), 0) == LISTED * lax.rem(l_col, Q)) & (rank == (l_col // Q).astype(F32)) & (l_col < VOFF)
    positive = tn(hold_b, pos_at.astype(F32).astype(BF16))
    valid = (count > (lane // Q).astype(F32)) & (lane < VOFF)

    row128 = iota((128, RANK), 0)
    at_rank = ((row128 >= VOFF) & (row128 < VOFF + SLOTS * RANK) & (lax.rem(row128 - VOFF + 128 * RANK, RANK) == iota((128, RANK), 1)))
    at_rank = at_rank.astype(F32)
    at_query = ((iota((Q, 128), 1) < VOFF) & (lax.rem(iota((Q, 128), 1), Q) == iota((Q, 128), 0))).astype(F32)
    spread = nn(nt(at_rank.astype(BF16), low_half).astype(BF16), at_query.astype(BF16))
    row_a, lane_a = iota((128, 128), 0), iota((128, 128), 1)
    same_slot = ((row_a + 128 * RANK - VOFF) // RANK - 128) == lane_a // Q
    spread = jnp.where(same_slot, spread, 0.0).astype(BF16)
    inv_lane = jnp.sum(inv_norm * at_query, axis=0, keepdims=True)

    for s in range(SLOTS):
        f_lane = iota((GROUP, 128), 1) - s * Q
        f_row = iota((GROUP, 128), 0)
        folds[0, s] = (f_lane == lax.rem(f_row, TALL)).astype(F32).astype(BF16)
        folds[1, s] = (f_lane == TALL + lax.rem(f_row, SHORT)).astype(F32).astype(BF16)
    take(got, got_sem)

    g = got[...].reshape(DEVS, 128)
    unshrink = jnp.sum(jnp.where(lane == G_LANE, g, 0.0), axis=1, keepdims=True)
    unshrink = jnp.where(unshrink < 0.5, 1.0 / TINY, 1.0)
    ranks = jnp.where((lane >= VOFF) & (lane < VOFF + SLOTS * RANK), g, 0.0)
    raw = g
    for piece in split(ranks, 3):
        raw = raw + nn(piece, spread)
    raw = jnp.where(valid & (inv_lane > 0.0), raw * inv_lane * unshrink, 0.0)
    scale = 1.0 / (SOFTMAX_TEMPER * math.sqrt(WIDTH * NX))
    scores = jnp.where(valid, raw * scale, NEG)

    def over_slots(x, op, fill):
        x0 = op(op(x, pltpu.roll(x, 128 - Q, 1)), pltpu.roll(x, 128 - 2 * Q, 1))
        return jnp.where(lane1 < Q, x0, jnp.where(lane1 < 2 * Q, pltpu.roll(x0, Q, 1), jnp.where(lane1 < 3 * Q, pltpu.roll(x0, 2 * Q, 1), fill)))

    top = over_slots(jnp.max(scores, axis=0, keepdims=True), jnp.maximum, 0.0)
    expo = jnp.where(valid, jnp.exp(scores - top), 0.0)
    total = over_slots(jnp.sum(expo, axis=0, keepdims=True), jnp.add, 1.0)
    own = over_slots(jnp.sum(jnp.where(positive > 0.5, scores, 0.0), axis=0, keepdims=True), jnp.add, 0.0)
    loss = jnp.sum(jnp.where(lane1 < Q, jnp.log(total) + top - own, 0.0), axis=1, keepdims=True)
    weights = jnp.where(valid, (expo / total - positive) * scale, 0.0)
    tangent = over_slots(jnp.sum(weights * raw, axis=0, keepdims=True), jnp.add, 0.0) / (WIDTH * NX)
    w2 = weights * inv_lane
    v = jnp.zeros((DEVS, 128), F32)
    for piece in split(w2, 3):
        v = v + nt(piece, spread)
    back[...] = (w2 + v + jnp.where(lane == LOSS_LANE, loss, 0.0)).reshape(2, CHIPS, 128)

    to_all(lambda chip, c: push(row_of(back, chip), row_of(wrec, chip_me), small_sem.at[8], w_sem, (chip * 2 + c, mp)), False)
    pltpu.make_async_copy(row_of(back, chip_me), row_of(wrec, chip_me), w_sem).start()

    z_all = exact(((0,), (0,)), weights, ranks * unshrink)
    z_all = jnp.where(lane_a >= VOFF, z_all, 0.0)
    same_t = ((lane_a + 128 * RANK - VOFF) // RANK - 128) == row_a // Q
    z_all = jnp.where(same_t, z_all, 0.0)
    w_pu = exact(((1,), (0,)), exact(((1,), (0,)), at_query, z_all), at_rank)
    inv_col = inv_norm[:, 0:1]
    q_up = inv_col * (hid_up + exact(((1,), (0,)), low_half.astype(F32), gram))
    tan_col = jnp.sum(jnp.where((iota((Q, 128), 1) < Q), at_query, 0.0) * tangent, axis=1, keepdims=True)
    low_grad = (inv_col * (w_pu - tan_col * q_up)).astype(BF16)
    ga = tn(low_grad, hidden_ref[...])
    pulled = (mixed_ref[...] * (inv_col * inv_col * tan_col)).astype(BF16)
    gb = -tn(low_half, pulled)

    for j in range(WIDTH // 128):
        piece_out[0, pl.ds(j * RANK, RANK), :] = ga[:, j * 128 : (j + 1) * 128]

    take(wrec, w_sem)
    w = wrec[...].reshape(DEVS, 128)
    lost = jnp.where((lane == LOSS_LANE) & (iota((DEVS, 128), 0) < CHIPS), w, 0.0)
    losses[core] = jnp.broadcast_to(jnp.sum(jnp.sum(lost, axis=0, keepdims=True), axis=1, keepdims=True), (8, 128))
    push(losses.at[core], losses.at[core], small_sem.at[13], loss_sem, sibling)
    w_t = jnp.transpose(w) * jnp.where(lane1 < CHIPS, 1.0 / flags[0, 0:1, :], 1.0 / flags[1, 0:1, :])
    for s in range(SLOTS):
        v_hi, v_lo = split(w_t[VOFF + s * RANK : VOFF + (s + 1) * RANK, :], 2)
        r = nn(jnp.concatenate([v_hi, v_lo], axis=0), slot_rows(s))
        gb = gb + r[0:RANK] + r[RANK : 2 * RANK]
    for j in range(WIDTH // 128):
        piece_out[1, pl.ds(j * RANK, RANK), :] = gb[:, j * 128 : (j + 1) * 128]

    to_all(lambda chip, c: push(row_of(piece_out, chip * 2 + c), row_of(piece_in, me), small_sem.at[9], rs_sem, (chip * 2 + c, mp)), True)
    pltpu.make_async_copy(piece_out.at[:, pl.ds(me, 1), :], piece_in.at[:, pl.ds(me, 1), :], rs_sem).start()

    hi, lo = split(w, 2)
    d_lane = iota((DEVS, GROUP), 1)
    wide = (d_lane // TALL) == lax.rem(iota((DEVS, GROUP), 0), 16)
    first_half = lax.rem(d_lane // SHORT, 2) == 0
    for s in range(SLOTS):
        for i, piece in enumerate((hi, lo)):
            diag[0, i, s] = jnp.where(wide, nt(piece, folds[0, s]), 0.0).astype(BF16)
            low8 = jnp.where(wide, nt(piece, folds[1, s]), 0.0)
            diag[1, i, s] = jnp.where(first_half, low8, 0.0).astype(BF16)
            diag[2, i, s] = jnp.where(first_half, 0.0, low8).astype(BF16)

    def candidates(g_, c):
        rows = pl.ds(pl.multiple_of(g_ * 16, 16), 16)
        d0, d1, d2 = (
            jnp.concatenate(
                [diag[n, i, s, pl.ds(pl.multiple_of(h * CHIPS + g_ * 16, 16), 16), :] for i in (0, 1) for h in (0, 1) for s in range(SLOTS)],
                axis=0,
            )
            for n in range(3)
        )
        o = nn(d0, tall(g_)) + jnp.concatenate([nn(d1, short(g_)), nn(d2, short(g_))], axis=1)
        o = o[0:SG, :] + o[SG : 2 * SG, :]
        for h in (0, 1):
            for s in range(SLOTS):
                at = (h * SLOTS + s) * 16
                cand[h, s, rows, :] = o[at : at + 16, :]
        return c

    lax.fori_loop(0, CHIPS // 16, candidates, 0)
    for s in range(SLOTS):
        up_at = up_lanes(s)
        cg = cand[:, s].reshape(DEVS, WIDTH) + nn(hi, up_at) + nn(lo, up_at)
        cand_out[:, s] = cg.astype(BF16).reshape(2, CHIPS, WIDTH)
    push(cand_out.at[1 - core], cand_all.at[core], small_sem.at[12], cand_sem, sibling)
    cand_all[core] = cand_out[core]

    take(piece_in, rs_sem)
    piece_sum[...] = jnp.sum(piece_in[...], axis=1, keepdims=True)
    final[:, pl.ds(me, 1), :] = piece_sum[...]

    to_all(lambda chip, c: push(piece_sum, row_of(final, me), small_sem.at[10], ag_sem, (chip * 2 + c, mp)), True)
    take(cand_all.at[0], cand_sem)
    table = jnp.zeros((ROWS, WIDTH), F32)
    for s in range(SLOTS):
        table = table + tn(pick[s], cand_all[:, s].reshape(DEVS, WIDTH))
    table_ref[...] = table.astype(BF16)
    table_out = pltpu.make_async_copy(table_ref, table_hbm, load_sem.at[6])
    table_out.start()

    take(final.at[:, pl.ds(0, DEVS - 1), :], ag_sem)
    pieces_ref[...] = final[...]
    take(losses.at[0], loss_sem)
    loss_ref[...] = (losses[0, 0:1, 0:1] + losses[1, 0:1, 0:1]) / (DEVS * Q)
    table_out.wait()

    take(hbuf.at[pl.ds(0, CHIPS - 1)], send_sem)
    take(picked.at[:, pl.ds(0, CHIPS), :], small_sem.at[0])
    take(xb1.at[pl.ds(0, NX - 1)], small_sem.at[1])
    take(lists.at[:, 0, pl.ds(0, 1), :], small_sem.at[2])
    take(xb2.at[pl.ds(0, NX - 1)], small_sem.at[3])
    take(lists.at[:, :, pl.ds(0, NZ - 1), :], small_sem.at[4])
    take(lists.at[:, :, pl.ds(0, NZ * (NY - 1)), :], small_sem.at[5])
    take(rsx.at[pl.ds(0, NX - 1)], small_sem.at[6])
    @pl.when(home)
    def _():
        take(got.at[:, pl.ds(0, CHIPS - 1), :], small_sem.at[7])

    @pl.when(jnp.logical_not(home))
    def _():
        take(got, small_sem.at[7])

    take(wrec.at[:, pl.ds(0, CHIPS - 1), :], small_sem.at[8])
    take(piece_in.at[:, pl.ds(0, DEVS - 1), :], small_sem.at[9])
    take(final.at[:, pl.ds(0, DEVS - 1), :], small_sem.at[10])
    take(flags.at[0], small_sem.at[11])
    take(losses.at[0], small_sem.at[13])
    take(cand_out.at[0], small_sem.at[12])


def finish(loss_in, pieces_ref, table_in, loss_ref, ga_ref, gb_ref, table_out):
    table_out[...] = table_in[...]

    @pl.when(pl.program_id(0) == 0)
    def _():
        loss_ref[...] = loss_in[...]
        for j in range(WIDTH // 128):
            ga_ref[:, pl.ds(j * 128, 128)] = pieces_ref[0, pl.ds(j * RANK, RANK), :]
            gb_ref[:, pl.ds(j * 128, 128)] = pieces_ref[1, pl.ds(j * RANK, RANK), :]


def shards(hidden, down, up, passages, ids, storage):
    vm, hbm = pl.BlockSpec(memory_space=pltpu.VMEM), pl.BlockSpec(memory_space=pl.ANY)
    dma = pltpu.SemaphoreType.DMA
    shape = jax.ShapeDtypeStruct
    loss, pieces, table = pl.pallas_call(
        kernel,
        out_shape=(shape((1, 1), F32), shape((2, DEVS, 128), F32), shape((ROWS, WIDTH), BF16)),
        in_specs=[hbm] * 6,
        out_specs=(vm, vm, hbm),
        scratch_shapes=[
            pltpu.SMEM((LISTED, Q), jnp.int32),
            pltpu.VMEM((Q, WIDTH), BF16),
            pltpu.VMEM((RANK, WIDTH), BF16),
            pltpu.VMEM((RANK, WIDTH), BF16),
            pltpu.VMEM((CHIPS, TALL, WIDTH + HALF), BF16),
            pltpu.VMEM((NX, 40, 128), F32),
            pltpu.VMEM((NX, Q, 128), F32),
            pltpu.VMEM((Q * LISTED, 128), F32),
            pltpu.VMEM((2, 2, CHIPS, 128), F32),
            pltpu.VMEM((SLOTS, DEVS, ROWS), BF16),
            pltpu.VMEM((SLOTS, DEVS, WIDTH), BF16),
            pltpu.VMEM((2, SLOTS, CHIPS, WIDTH), BF16),
            pltpu.VMEM((2, 8, 128), F32),
            pltpu.VMEM((2, 8, 128), F32),
            pltpu.VMEM((2, SLOTS, GROUP, 128), BF16),
            pltpu.VMEM((3, 2, SLOTS, DEVS, GROUP), BF16),
            pltpu.VMEM((NX, 2, CHIPS // NX, 128), F32),
            pltpu.VMEM((2, CHIPS, 128), F32),
            pltpu.VMEM((2, CHIPS // NX, 128), F32),
            pltpu.VMEM((2, CHIPS, 128), F32),
            pltpu.VMEM((2, CHIPS, 128), F32),
            pltpu.VMEM((2, CHIPS, 128), F32),
            pltpu.VMEM((2, SLOTS, CHIPS, WIDTH), F32),
            pltpu.VMEM((2, SLOTS, CHIPS, WIDTH), BF16),
            pltpu.VMEM((2, SLOTS, CHIPS, WIDTH), BF16),
            pltpu.VMEM((2, DEVS, 128), F32),
            pltpu.VMEM((2, DEVS, 128), F32),
            pltpu.VMEM((2, 1, 128), F32),
            pltpu.VMEM((2, DEVS, 128), F32),
            pltpu.VMEM((Q, WIDTH), F32),
            pltpu.VMEM((ROWS, WIDTH), BF16),
            pltpu.VMEM((ROWS, 128), jnp.int32),
            pltpu.VMEM((ROWS, WIDTH), BF16),
            dma, dma, dma,
            dma((NZ,)), dma((NY,)),
            dma((CHIPS,)), dma, dma, dma, dma,
            dma, dma, dma, dma, dma,
            dma, dma((14,)), dma((7,)),
        ],
        compiler_params=pltpu.CompilerParams(collective_id=0, has_side_effects=True, vmem_limit_bytes=56 << 20),
        name="contrastive",
    )(ids.T, hidden, down, up, passages, storage.reshape(ROWS, 128))
    rows = pl.BlockSpec((ROWS // 2, WIDTH), lambda i: (i, 0))

    def whole(*dims):
        return pl.BlockSpec(dims, lambda i: (0,) * len(dims))

    loss, ga, gb, table = pl.pallas_call(
        finish,
        out_shape=(shape((1, 1), F32), shape((RANK, WIDTH), F32), shape((RANK, WIDTH), F32), shape((ROWS, WIDTH), BF16)),
        grid=(2,),
        in_specs=[whole(1, 1), whole(2, DEVS, 128), rows],
        out_specs=(whole(1, 1), whole(RANK, WIDTH), whole(RANK, WIDTH), rows),
        name="finish",
    )(loss, pieces, table)
    return loss.reshape(()), ga, gb, table


def solution(mesh):
    return jax.shard_map(
        shards,
        mesh=mesh,
        in_specs=(P("dp", "mp"), P(None, "mp"), P(None, "mp"), P("dp", "mp"), P("dp", None), P()),
        out_specs=(P(), P(None, "mp"), P(None, "mp"), P("dp", "mp")),
        check_vma=False,
    )
```
